256 devices in a mesh: gz: 4 (over z_hi, core), xy: 64 (over y, x, z_lo).
Axes of the slice: x: 4, y: 4, z: 8 (z_hi: 2, z_lo: 4; z = z_hi * 4 + z_lo), core: 2. Of those that a mesh axis runs over, the one named last changes fastest.
Arguments:
- left_vectors: float32 [3, 8, 16, 16, 64, 256], P(None, None, None, 'gz', 'xy'), may hold values from -6 to 6
- sign_seeds: int32 [16], replicated, may hold values from 0 to 16777215
- level_codes: int32 [16, 64, 256], P('gz', 'xy'), may hold values from 0 to 3
- level_table: float32 [4], replicated, may hold values from -1.5 to 1.5
- disorder_sites: int32 [4096], replicated, may hold values from 0 to 262143
- disorder_strength: float32 [4096], replicated, may hold values from -3 to 3
- hoppings: float32 [3, 8, 8], replicated, may hold values from -1.5 to 1.5
- mass_raw: float32 [8, 8], replicated, may hold values from -3 to 3
Outputs:
- moments: float32 [3, 4, 16], replicated
- cheb_prev: float32 [8, 16, 16, 64, 256], P(None, None, 'gz', 'xy')
- cheb_last: float32 [8, 16, 16, 64, 256], P(None, None, 'gz', 'xy')
The draws below stay inside these ranges and needn't reach their ends.
All inputs are finite; a program needn't handle non-finite values.
Results may differ from the reference program's by a relative error of at most 0.0011.
Values may be sent and summed in bfloat16 or wider, within the bound.
A program may use at most 64 MiB of HBM per device.

```python
import math
import jax
import jax.numpy as jnp
from jax import lax

ORB = 8
PANEL = 16
LEFT = 3
STEPS = 3
LEVELS = 4
TY = 8
CX = 16
CY = 16
AREA = 256
TX = 8
TILES = 64
NZ = 16
NX = 128
NY = 128
CELLS = 262144
NDIS = 4096


def set_ends(drawn, key, least, top_value):
    longest = drawn.shape.index(max(drawn.shape))
    spots = []
    for shift in (0, 1):
        where = [jax.random.randint(jax.random.fold_in(key, axis), (), 0, length) for axis, length in enumerate(drawn.shape)]
        where[longest] = (where[longest] + shift) % drawn.shape[longest]
        spots.append(tuple(where))
    return drawn.at[spots[0]].set(least).at[spots[1]].set(top_value)


def block_scale(key, extent, shards, least, top_value):
    def one(position, blocks):
        draws = jax.random.uniform(jax.random.fold_in(jax.random.fold_in(key, 6), position), (blocks,), jnp.float32, least / len(shards), top_value / len(shards))
        return jnp.repeat(jnp.exp(draws), extent[position] // blocks).reshape((-1,) + (1,) * (len(extent) - position - 1))

    level = one(*shards[0])
    for cut in shards[1:]:
        level = level * one(*cut)
    return level


def bell_draw(stream_key, shape, scale, reach, shards=(), kind=jnp.bfloat16):
    array = scale * jax.random.normal(stream_key, shape, jnp.float32)
    if shards:
        array = array * block_scale(stream_key, shape, shards, -0.22, 0.18)
    return jnp.clip(array, -reach, reach).astype(kind)


def setup_inputs(seed: int = 0) -> dict:
    splits = jax.random.split(jax.random.key(seed), 9)
    return {
        "left_vectors": bell_draw(splits[0], (LEFT, ORB, PANEL, NZ, TILES, AREA), 1.0, 6.0, ((3, 4), (4, 64)), jnp.float32),
        "sign_seeds": set_ends(jax.random.randint(splits[1], (PANEL,), 0, 16777216), jax.random.fold_in(splits[1], 1), 0, 16777215).astype(jnp.int32),
        "level_codes": set_ends(jax.random.randint(splits[2], (NZ, TILES, AREA), 0, LEVELS), jax.random.fold_in(splits[2], 1), 0, LEVELS - 1).astype(jnp.int32),
        "level_table": jnp.clip(jax.random.uniform(splits[3], (LEVELS,), jnp.float32, -1.5, 1.5), -1.5, 1.5),
        "disorder_sites": set_ends(jax.random.randint(splits[4], (NDIS,), 0, CELLS), jax.random.fold_in(splits[4], 1), 0, CELLS - 1).astype(jnp.int32),
        "disorder_strength": jnp.clip(jax.random.uniform(splits[5], (NDIS,), jnp.float32, -3.0, 3.0), -3.0, 3.0),
        "hoppings": bell_draw(splits[6], (3, ORB, ORB), 16 ** -0.5, 1.5, (), jnp.float32),
        "mass_raw": bell_draw(splits[7], (ORB, ORB), 0.5, 3.0, (), jnp.float32),
    }


energy_scale = 5.0
highest = lax.Precision.HIGHEST

def orbital_product(matrix, values):
    return jnp.einsum('ab,...bqzxy->...aqzxy', matrix, values, precision=highest)

def to_grid(values):
    leading = tuple(values.shape[:-2])
    count_before = len(leading)
    pieces = values.reshape(leading + (TX, TY, CX, CY))
    permuted = tuple(range(count_before)) + (count_before, count_before + 2, count_before + 1, count_before + 3)
    return pieces.transpose(permuted).reshape(leading + (NX, NY))

def to_tiles(values):
    leading = tuple(values.shape[:-2])
    count_before = len(leading)
    pieces = values.reshape(leading + (TX, CX, TY, CY))
    permuted = tuple(range(count_before)) + (count_before, count_before + 2, count_before + 1, count_before + 3)
    return pieces.transpose(permuted).reshape(leading + (TILES, AREA))

def hashed_signs(sign_seeds, cell_ids, orbitals):
    orbital_ids = lax.broadcasted_iota(jnp.int32, (orbitals, 1, 1, 1, 1), 0)
    flat_index = cell_ids[None, None] * orbitals + orbital_ids
    scrambled = flat_index * 668265261 + sign_seeds[None, :, None, None, None]
    scrambled = scrambled ^ lax.shift_right_logical(scrambled, jnp.int32(15))
    scrambled = scrambled * -2048144789
    scrambled = scrambled ^ lax.shift_right_logical(scrambled, jnp.int32(13))
    scrambled = scrambled * -1028477387
    scrambled = scrambled ^ lax.shift_right_logical(scrambled, jnp.int32(16))
    top_bit = lax.shift_right_logical(scrambled, jnp.int32(31))
    return (1 - 2 * top_bit).astype(jnp.float32).astype(jnp.bfloat16)

def open_step(values, axis_num, forward):
    size_along = values.shape[axis_num]
    padding = [(0, 0)] * values.ndim
    padding[axis_num] = (0, 1) if forward else (1, 0)
    padded = jnp.pad(values, padding)
    begin = 1 if forward else 0
    return lax.slice_in_dim(padded, begin, begin + size_along, axis=axis_num)

def hamiltonian(values, onsite, hoppings, mass):
    result = orbital_product(mass, values) + onsite * values
    result = result + orbital_product(hoppings[0], jnp.roll(values, -1, axis=3)) + orbital_product(hoppings[0].T, jnp.roll(values, 1, axis=3))
    result = result + orbital_product(hoppings[1], open_step(values, 4, True)) + orbital_product(hoppings[1].T, open_step(values, 4, False))
    result = result + orbital_product(hoppings[2], jnp.roll(values, -1, axis=2)) + orbital_product(hoppings[2].T, jnp.roll(values, 1, axis=2))
    return result

def velocity(matrix, values, axis_num):
    return orbital_product(matrix, jnp.roll(values, -1, axis=axis_num)) - orbital_product(matrix.T, jnp.roll(values, 1, axis=axis_num))

def reference(left_vectors, sign_seeds, level_codes, level_table, disorder_sites, disorder_strength, hoppings, mass_raw):
    z_coord = jnp.arange(NZ, dtype=jnp.int32)
    x_coord = jnp.arange(NX, dtype=jnp.int32)
    y_coord = jnp.arange(NY, dtype=jnp.int32)
    cell_ids = (z_coord[:, None, None] * NX + x_coord[None, :, None]) * NY + y_coord[None, None, :]
    signs = hashed_signs(sign_seeds, cell_ids, ORB)
    codes_grid = to_grid(level_codes)
    level_ids = jnp.arange(LEVELS, dtype=jnp.int32)
    one_hot = (codes_grid[None] == level_ids[:, None, None, None]).astype(jnp.float32)
    base_level = lax.optimization_barrier(jnp.sum(one_hot * level_table[:, None, None, None], axis=0))
    onsite = base_level.reshape(-1).at[disorder_sites].add(disorder_strength).reshape(NZ, NX, NY)
    mass = 0.5 * (mass_raw + mass_raw.T)
    left_grid = to_grid(left_vectors)
    current = velocity(hoppings[0], signs.astype(jnp.float32), 3)
    cheb_chain = [current]
    for step_num in range(STEPS):
        applied = hamiltonian(cheb_chain[-1], onsite, hoppings, mass)
        if step_num == 0:
            cheb_chain.append(applied * (1.0 / energy_scale))
        else:
            cheb_chain.append(applied * (2.0 / energy_scale) - cheb_chain[-2])
    local_tiles = []
    for vector_n in cheb_chain:
        probe = velocity(hoppings[2], vector_n, 2)
        local_tiles.append(jnp.einsum('morzxy,orzxy->mr', left_grid, probe, precision=highest))
    moments = jnp.stack(local_tiles, axis=1) * (1.0 / math.sqrt(ORB * CELLS))
    return (moments, to_tiles(cheb_chain[-2]), to_tiles(cheb_chain[-1]))
```

```python
import functools
import math

import jax
import jax.numpy as jnp
from jax import lax
from jax.experimental import pallas as pl
from jax.experimental.pallas import tpu as pltpu
from jax.sharding import PartitionSpec as P

f32, bf16, i32 = jnp.float32, jnp.bfloat16, jnp.int32

PITCH = 24
NR = 608
LOHI = {0: (112, 496), 1: (80, 512), 2: (64, 544), 3: (32, 560)}
MULT = 668265261
NT = (((1,), (1,)), ((), ()))
highest = lax.Precision.HIGHEST


def split2(v):
    hi = v.astype(bf16)
    lo = (v - hi.astype(f32)).astype(bf16)
    return hi, lo


def split3(v):
    hi = v.astype(bf16)
    rest = v - hi.astype(f32)
    mid = rest.astype(bf16)
    lo = (rest - mid.astype(f32)).astype(bf16)
    return hi, mid, lo


def iota(shape, dim):
    return lax.broadcasted_iota(i32, shape, dim)


def rows_to_xy(rows):
    i = rows - 12
    q = lax.shift_right_arithmetic(i * 2731, jnp.full(i.shape, 16, i32))
    return q - 4, i - q * 24 - 4


def own_rows(block, lo):
    return jnp.concatenate(
        [block[112 + 24 * x - lo : 112 + 24 * x - lo + 16] for x in range(16)], axis=0
    )


def wrap32(value):
    value &= 0xFFFFFFFF
    return value - (1 << 32) if value >= (1 << 31) else value


def chain_kernel(
    place,
    seed_ref,
    hop_ref,
    mass_ref,
    on_ref,
    left_ref,
    prev_ref,
    last_ref,
    part_ref,
    wm_ref,
    wy_ref,
    w0_ref,
    wz_ref,
    hb_ref,
    mk_ref,
    sb_ref,
    f0_ref,
    f1_ref,
    f2_ref,
    a0_ref,
    a1_ref,
    a2_ref,
    b0_ref,
    b1_ref,
    b2_ref,
    c_ref,
    obc_ref,
    ob_ref,
    acc_ref,
):
    gz, tx, ty = place()

    lane8 = iota((8, 128), 1)
    spread = jnp.where(lax.shift_right_logical(lane8, 4) == iota((8, 128), 0), 1.0, 0.0)
    mass_raw = mass_ref[...]
    mass = 0.5 * (mass_raw + mass_raw.T)
    mats = [mass]
    for d in range(3):
        mats += [hop_ref[d].T, hop_ref[d]]
    stack = jnp.concatenate(mats, axis=0) * 0.4
    wide = jnp.dot(stack, spread, precision=highest, preferred_element_type=f32)
    same_r = (iota((16, 128), 1) & 15) == iota((16, 128), 0)
    full = []
    for k in range(7):
        blocks = []
        for b in range(8):
            row = wide[8 * k + b : 8 * k + b + 1]
            blocks.append(jnp.where(same_r, jnp.broadcast_to(row, (16, 128)), 0.0))
        full.append(split2(jnp.concatenate(blocks, axis=0)))
    for slot, k in enumerate((0, 1, 2, 5, 6)):
        both = jnp.concatenate(full[k], axis=1)
        wm_ref[256 * slot : 256 * slot + 128] = both
        wm_ref[256 * slot + 128 : 256 * slot + 256] = both
    for part in range(2):
        both = jnp.concatenate([full[3][part], full[4][part]], axis=1)
        wy_ref[256 * part : 256 * part + 128] = both
        wy_ref[256 * part + 128 : 256 * part + 256] = both
    w0_ref[0:128] = jnp.concatenate(full[1], axis=1)
    w0_ref[128:256] = -jnp.concatenate(full[2], axis=1)
    for part in range(2):
        wz_ref[128 * part : 128 * part + 128] = jnp.concatenate(
            [full[6][part], full[6][part], -full[5][part], -full[5][part]], axis=1
        )

    x, y = rows_to_xy(iota((576, 128), 0) + 8)
    lane = iota((576, 128), 1)
    xg = (tx * 16 + x + 128) & 127
    yg = ty * 16 + y
    lane1 = iota((1, 128), 1) & 15
    seeds = jnp.zeros((1, 128), i32)
    for r in range(16):
        seeds = jnp.where(lane1 == r, seed_ref[r], seeds)
    hb_ref[...] = ((xg * 128 + yg) * 8 + lax.shift_right_logical(lane, 4)) * MULT + seeds
    mk_ref[...] = jnp.where((yg >= 0) & (yg < 128), 1.0, 0.0)

    obc_ref[...] = jnp.zeros(obc_ref.shape, f32)
    for dx, h, lo, hi in ((0, 0, 96, 304), (0, 1, 288, 496), (-1, 1, 64, 112), (1, 0, 480, 544)):
        xr, yr = rows_to_xy(iota((hi - lo, 128), 0) + lo)
        xr = xr - 16 * dx - 8 * h
        ok = (xr >= 0) & (xr < 8)
        lane = iota((hi - lo, 128), 1)
        sels, vals = [], []
        for dy in (-1, 0, 1):
            yy = yr - 16 * dy
            hit = ok & (yy >= 0) & (yy < 16) & (xr * 16 + yy == lane)
            sel = jnp.where(hit, 1.0, 0.0).astype(bf16)
            for piece in split3(on_ref[(dx + 1) * 3 + dy + 1, h]):
                sels.append(sel)
                vals.append(piece)
        obc_ref[lo - 64 : hi - 64] += lax.dot_general(
            jnp.concatenate(sels, axis=1),
            jnp.concatenate(vals, axis=1),
            NT,
            preferred_element_type=f32,
        )
    for p in range(1, 11):
        col = (p // 4) * 8 + p % 4
        ob_ref[p - 1] = jnp.broadcast_to(obc_ref[:, col : col + 1] * 0.4, (480, 128))

    def sign_plane(p, carry):
        zg = (gz * 4 + p + 12) & 15
        word = hb_ref[...] + zg * wrap32(128 * 128 * 8 * MULT)
        word = word ^ lax.shift_right_logical(word, jnp.full(word.shape, 15, i32))
        word = word * -2048144789
        word = word ^ lax.shift_right_logical(word, jnp.full(word.shape, 13, i32))
        word = word * -1028477387
        mk = mk_ref[...]
        sb_ref[p] = jnp.where(word < 0, -mk, mk).astype(bf16)
        return carry

    lax.fori_loop(0, 12, sign_plane, 0)

    def keep(level, p, out, lo, hi):
        f_ref, a_ref, b_ref = ((f0_ref, a0_ref, b0_ref), (f1_ref, a1_ref, b1_ref), (f2_ref, a2_ref, b2_ref))[level]
        f_ref[p, lo:hi] = out
        hi_f = out.astype(bf16).astype(f32)
        lo_f = out - hi_f
        both = jnp.concatenate([hi_f, lo_f], axis=1)
        a_ref[p, lo:hi] = both.astype(bf16)
        b_ref[p, lo - 16 : hi] = jnp.concatenate([both[:8], both, both[:8]], axis=0).astype(bf16)
        return both

    def for_planes(level, radius, body):
        lo, hi = LOHI[radius]
        inner = functools.partial(body, lo=lo, hi=hi, own=True)
        lax.fori_loop(3, 9, lambda p, c: (inner(p), c)[1], 0)
        for k in range(1, radius + 1):
            lo, hi = LOHI[radius - k]
            outer = functools.partial(body, lo=lo, hi=hi, own=False)
            lax.fori_loop(0, 2, lambda i, c: (outer(3 - k + i * (5 + 2 * k)), c)[1], 0)

    def start(p, lo, hi, own):
        lhs = jnp.concatenate([sb_ref[p, lo + 16 : hi + 16], sb_ref[p, lo - 32 : hi - 32]], axis=1)
        prod = jnp.dot(lhs, w0_ref[...], preferred_element_type=f32)
        out = (prod[:, :128] + prod[:, 128:]) * 2.5
        both = keep(0, p, out, lo, hi)
        if own:
            c_ref[0, p - 3] = own_rows(both, lo).astype(bf16)

    for_planes(0, 3, start)

    fs = (f0_ref, f1_ref, f2_ref)
    as_ = (a0_ref, a1_ref, a2_ref)
    bs = (b0_ref, b1_ref, b2_ref)

    def step(n, p, lo, hi, own):
        a_ref, b_ref = as_[n], bs[n]
        lhs = jnp.concatenate(
            [
                a_ref[p, lo:hi],
                b_ref[p, lo + 16 : hi + 16],
                b_ref[p, lo - 32 : hi - 32],
                a_ref[p + 1, lo:hi],
                a_ref[p - 1, lo:hi],
            ],
            axis=1,
        )
        main = jnp.dot(lhs, wm_ref[...], preferred_element_type=f32)
        size = hi - lo + 16
        first = 0 if (lo, hi) == LOHI[1] else 16
        ylhs = a_ref[p, lo - first : lo - first + size]
        yy = jnp.dot(jnp.concatenate([ylhs, ylhs], axis=1), wy_ref[...], preferred_element_type=f32)
        yp = pltpu.roll(yy[:, :128], size - 1, 0)[first : first + hi - lo]
        ym = pltpu.roll(yy[:, 128:], 1, 0)[first : first + hi - lo]
        out = main[:, :128] + main[:, 128:] + yp + ym + ob_ref[p - 1, lo - 64 : hi - 64] * fs[n][p, lo:hi]
        out = out * mk_ref[lo - 8 : hi - 8]
        if n == 0:
            out = out * 0.5
        else:
            out = out - fs[n - 1][p, lo:hi]
        return out

    def step_keep(n, p, lo, hi, own):
        both = keep(n + 1, p, step(n, p, lo, hi, own), lo, hi)
        if own:
            c_ref[n + 1, p - 3] = own_rows(both, lo).astype(bf16)

    for_planes(1, 2, functools.partial(step_keep, 0))
    for_planes(2, 1, functools.partial(step_keep, 1))

    def step_last(p, lo, hi, own):
        out = step(2, p, lo, hi, own)
        v = own_rows(out, lo)
        hi_f = v.astype(bf16).astype(f32)
        c_ref[3, p - 3] = jnp.concatenate([hi_f, v - hi_f], axis=1).astype(bf16)
        f0_ref[p, 0:256] = v

    for_planes(3, 0, step_last)

    acc_ref[...] = jnp.zeros(acc_ref.shape, f32)

    def plane_out(z, carry):
        p = z + 4
        last = f0_ref[p, 0:256].T
        prev = own_rows(f2_ref[p, 80:512], 80).T
        for h in range(2):
            last_ref[pl.ds(2 * z + h, 128, stride=8), :] = last[:, 128 * h : 128 * h + 128]
            prev_ref[pl.ds(2 * z + h, 128, stride=8), :] = prev[:, 128 * h : 128 * h + 128]
        us = []
        for n in range(4):
            rhs = jnp.concatenate([c_ref[n, z + 2], c_ref[n, z]], axis=1)
            u = lax.dot_general(wz_ref[...], rhs, NT, preferred_element_type=f32)
            us.append(u[:128] + u[128:])
        for h in range(2):
            for m in range(3):
                lv = left_ref[m, pl.ds(2 * z + h, 128, stride=8), :]
                for n in range(4):
                    prod = lv * us[n][:, 128 * h : 128 * h + 128]
                    tot = prod[0:16]
                    for o in range(1, 8):
                        tot = tot + prod[16 * o : 16 * o + 16]
                    acc_ref[m * 4 + n] += tot
        return carry

    lax.fori_loop(0, 4, plane_out, 0)
    lanes = iota((8, 128), 1)
    part = jnp.zeros((8, 128), f32)
    for k in range(12):
        tot = jnp.sum(acc_ref[k], axis=1, keepdims=True)
        part = jnp.where(lanes == k, tot[0:8], part)
        part = jnp.where(lanes == k + 16, tot[8:16], part)
    part_ref[...] = part * (2.5 / math.sqrt(8 * 262144))


def chain(place, seeds, hoppings, mass_raw, on_halo, left):
    vm = pl.BlockSpec(memory_space=pltpu.VMEM)
    plane = lambda kind, lanes: pltpu.VMEM((12, NR, lanes), kind)
    return pl.pallas_call(
        functools.partial(chain_kernel, place),
        out_shape=(
            jax.ShapeDtypeStruct((1024, 128), f32),
            jax.ShapeDtypeStruct((1024, 128), f32),
            jax.ShapeDtypeStruct((8, 128), f32),
        ),
        in_specs=[pl.BlockSpec(memory_space=pltpu.SMEM), vm, vm, vm, vm],
        out_specs=(vm, vm, vm),
        scratch_shapes=[
            pltpu.VMEM((1280, 256), bf16),
            pltpu.VMEM((512, 256), bf16),
            pltpu.VMEM((256, 256), bf16),
            pltpu.VMEM((256, 512), bf16),
            pltpu.VMEM((576, 128), i32),
            pltpu.VMEM((576, 128), f32),
            pltpu.VMEM((12, 576, 128), bf16),
            plane(f32, 128),
            plane(f32, 128),
            plane(f32, 128),
            plane(bf16, 256),
            plane(bf16, 256),
            plane(bf16, 256),
            plane(bf16, 256),
            plane(bf16, 256),
            plane(bf16, 256),
            pltpu.VMEM((4, 6, 256, 256), bf16),
            pltpu.VMEM((480, 32), f32),
            pltpu.VMEM((10, 480, 128), f32),
            pltpu.VMEM((12, 16, 128), f32),
        ],
        compiler_params=pltpu.CompilerParams(vmem_limit_bytes=56 * 1024 * 1024),
        name="chain",
    )(seeds, hoppings, mass_raw, on_halo, left)


def where_am_i():
    tile = lax.axis_index("xy")
    return lax.axis_index("gz"), tile // 8, tile % 8


def onsite_kernel(codes_ref, table_ref, sites_ref, strength_ref, halo_ref, send_sem, recv_sem):
    gz, tx, ty = where_am_i()
    offsets = [(dx, dy, dz) for dx in (-1, 0, 1) for dy in (-1, 0, 1) for dz in (-1, 0, 1)]
    offsets = [o for o in offsets if o != (0, 0, 0)]

    def device(dx, dy, dz):
        tile = ((tx + dx + 8) % 8) * 8 + (ty + dy + 8) % 8
        return {"gz": (gz + dz + 4) % 4, "xy": tile}

    halo_ref[...] = jnp.zeros(halo_ref.shape, f32)
    barrier = pltpu.get_barrier_semaphore()
    for o in offsets:
        pl.semaphore_signal(barrier, inc=1, device_id=device(*o), device_id_type=pl.DeviceIdType.MESH)

    codes = codes_ref[...]
    base = jnp.zeros((8, 128), f32)
    for level in range(4):
        base = jnp.where(codes == level, table_ref[level], base)
    site = sites_ref[...]
    lz = (site >> 14) - gz * 4
    lx = ((site >> 7) & 127) - tx * 16
    ly = (site & 127) - ty * 16
    inside = (lz >= 0) & (lz < 4) & (lx >= 0) & (lx < 16) & (ly >= 0) & (ly < 16)
    row = jnp.where(inside, lz * 2 + (lx >> 3), -1)
    col = (lx & 7) * 16 + ly
    pieces = split3(strength_ref[...])
    lhs, rhs = [], []
    for k in range(32):
        hit = jnp.broadcast_to(row[k : k + 1], (8, 128)) == iota((8, 128), 0)
        lhs.append(
            jnp.concatenate(
                [jnp.where(hit, jnp.broadcast_to(p[k : k + 1].astype(f32), (8, 128)), 0.0) for p in pieces]
                + [jnp.zeros((8, 128), f32)],
                axis=0,
            ).astype(bf16)
        )
        at = jnp.broadcast_to(col[k : k + 1], (128, 128)) == iota((128, 128), 0)
        rhs.append(jnp.where(at, 1.0, 0.0).astype(bf16))
    added = lax.dot_general(
        jnp.concatenate(lhs, axis=1), jnp.concatenate(rhs, axis=1), NT, preferred_element_type=f32
    )
    onsite = base + (added[0:8] + added[8:16] + added[16:24])
    for z in range(4):
        for h in range(2):
            halo_ref[4, h, 8 + z : 9 + z] = onsite[2 * z + h : 2 * z + h + 1]

    pl.semaphore_wait(barrier, len(offsets))
    copies = []
    mine = halo_ref.at[4, :, pl.ds(8, 8)]
    for k, (dx, dy, dz) in enumerate(offsets):
        copy = pltpu.make_async_remote_copy(
            src_ref=mine,
            dst_ref=halo_ref.at[(1 - dx) * 3 + 1 - dy, :, pl.ds(8 * (1 - dz), 8)],
            send_sem=send_sem.at[k],
            recv_sem=recv_sem.at[k],
            device_id=device(dx, dy, dz),
            device_id_type=pl.DeviceIdType.MESH,
        )
        copy.start()
        copies.append(copy)
    for copy in copies:
        copy.wait()


def onsite_halo(level_codes, level_table, sites, strength):
    vm = pl.BlockSpec(memory_space=pltpu.VMEM)
    return pl.pallas_call(
        onsite_kernel,
        out_shape=jax.ShapeDtypeStruct((9, 2, 32, 128), f32),
        in_specs=[vm, pl.BlockSpec(memory_space=pltpu.SMEM), vm, vm],
        out_specs=vm,
        scratch_shapes=[pltpu.SemaphoreType.DMA((26,)), pltpu.SemaphoreType.DMA((26,))],
        compiler_params=pltpu.CompilerParams(
            collective_id=0, has_side_effects=True, vmem_limit_bytes=16 * 1024 * 1024
        ),
        name="onsite",
    )(level_codes, level_table, sites, strength)


def total_kernel(part_ref, out_ref, got_ref, mid_ref, send_sem, recv_sem):
    gz = lax.axis_index("gz")
    tile = lax.axis_index("xy")
    zpos = gz * 4 + tile % 4
    plane = tile // 4

    def along_z(step):
        other = (zpos + step) % 16
        return {"gz": other // 4, "xy": plane * 4 + other % 4}

    def along_plane(step):
        return {"gz": gz, "xy": ((plane + step) % 16) * 4 + tile % 4}

    barrier = pltpu.get_barrier_semaphore()
    for step in range(1, 16):
        for device in (along_z(step), along_plane(step)):
            pl.semaphore_signal(barrier, inc=1, device_id=device, device_id_type=pl.DeviceIdType.MESH)
    pl.semaphore_wait(barrier, 30)
    value = part_ref
    for stage, target in enumerate((along_z, along_plane)):
        copies = []
        for step in range(1, 16):
            copy = pltpu.make_async_remote_copy(
                src_ref=value,
                dst_ref=got_ref.at[stage, step - 1],
                send_sem=send_sem.at[stage, step - 1],
                recv_sem=recv_sem.at[stage, step - 1],
                device_id=target(step),
                device_id_type=pl.DeviceIdType.MESH,
            )
            copy.start()
            copies.append(copy)
        for copy in copies:
            copy.wait()
        total = value[...]
        for step in range(1, 16):
            total = total + got_ref[stage, step - 1]
        mid_ref[...] = total
        value = mid_ref
    flat = jnp.concatenate([total, jnp.zeros((120, 128), f32)], axis=0).T
    for m in range(3):
        out_ref[m, :, 0:8] = flat[4 * m : 4 * m + 4, 0:8]
        out_ref[m, :, 8:16] = flat[16 + 4 * m : 20 + 4 * m, 0:8]


def total(part):
    vm = pl.BlockSpec(memory_space=pltpu.VMEM)
    return pl.pallas_call(
        total_kernel,
        out_shape=jax.ShapeDtypeStruct((3, 4, 16), f32),
        in_specs=[vm],
        out_specs=vm,
        scratch_shapes=[
            pltpu.VMEM((2, 15, 8, 128), f32),
            pltpu.VMEM((8, 128), f32),
            pltpu.SemaphoreType.DMA((2, 15)),
            pltpu.SemaphoreType.DMA((2, 15)),
        ],
        compiler_params=pltpu.CompilerParams(
            collective_id=1, has_side_effects=True, vmem_limit_bytes=16 * 1024 * 1024
        ),
        name="total",
    )(part)


def per_device(
    left_vectors,
    sign_seeds,
    level_codes,
    level_table,
    disorder_sites,
    disorder_strength,
    hoppings,
    mass_raw,
):
    halo = onsite_halo(
        level_codes.reshape(8, 128),
        level_table,
        disorder_sites.reshape(32, 128),
        disorder_strength.reshape(32, 128),
    )
    prev, last, part = chain(
        where_am_i, sign_seeds, hoppings, mass_raw, halo, left_vectors.reshape(3, 1024, 128)
    )
    shape = left_vectors.shape[1:]
    return total(part), prev.reshape(shape), last.reshape(shape)


def solution(mesh):
    in_specs = (
        P(None, None, None, "gz", "xy", None),
        P(),
        P("gz", "xy", None),
        P(),
        P(),
        P(),
        P(),
        P(),
    )
    out_specs = (P(), P(None, None, "gz", "xy", None), P(None, None, "gz", "xy", None))
    return jax.shard_map(
        per_device, mesh=mesh, in_specs=in_specs, out_specs=out_specs, check_vma=False
    )
```

```python
import functools
import math

import jax
import jax.numpy as jnp
from jax import lax
from jax.experimental import pallas as pl
from jax.experimental.pallas import tpu as pltpu
from jax.sharding import PartitionSpec as P

f32, bf16, i32 = jnp.float32, jnp.bfloat16, jnp.int32

PITCH = 24
NR = 608
LOHI = {0: (112, 496), 1: (80, 512), 2: (64, 544), 3: (32, 560)}
MULT = 668265261
NT = (((1,), (1,)), ((), ()))
highest = lax.Precision.HIGHEST


def split2(v):
    hi = v.astype(bf16)
    lo = (v - hi.astype(f32)).astype(bf16)
    return hi, lo


def split3(v):
    hi = v.astype(bf16)
    rest = v - hi.astype(f32)
    mid = rest.astype(bf16)
    lo = (rest - mid.astype(f32)).astype(bf16)
    return hi, mid, lo


def iota(shape, dim):
    return lax.broadcasted_iota(i32, shape, dim)


def rows_to_xy(rows):
    i = rows - 12
    q = lax.shift_right_arithmetic(i * 2731, jnp.full(i.shape, 16, i32))
    return q - 4, i - q * 24 - 4


def own_rows(block, lo):
    return jnp.concatenate(
        [block[112 + 24 * x - lo : 112 + 24 * x - lo + 16] for x in range(16)], axis=0
    )


def wrap32(value):
    value &= 0xFFFFFFFF
    return value - (1 << 32) if value >= (1 << 31) else value


def groups_of(radius):
    sets = [(2, lambda i: [3 + 3 * i, 4 + 3 * i, 5 + 3 * i], LOHI[radius], True)]
    for k in range(1, radius + 1):
        sets.append((1, lambda i, k=k: [3 - k, 8 + k], LOHI[radius - k], False))
    return sets


def each_group(radius, body):
    for count, planes, (lo, hi), own in groups_of(radius):
        if count == 1:
            body(planes(0), lo, hi, own)
        else:
            lax.fori_loop(0, count, lambda i, c: (body(planes(i), lo, hi, own), c)[1], 0)


def rows(parts):
    return jnp.concatenate(parts, axis=0)


def lanes_of(parts):
    return jnp.concatenate(parts, axis=1)


def kernel(
    place,
    comm,
    seed_ref,
    hop_ref,
    mass_ref,
    codes_ref,
    table_ref,
    sites_ref,
    strength_ref,
    left_hbm,
    *refs,
):
    if not comm:
        halo_in, refs = refs[0], refs[1:]
    (
        moments_ref,
        prev_ref,
        last_ref,
        halo_ref,
        left_ref,
        wm_ref,
        wy_ref,
        w0_ref,
        wz_ref,
        hb_ref,
        mk_ref,
        sb_ref,
        f0_ref,
        f1_ref,
        f2_ref,
        a0_ref,
        a1_ref,
        a2_ref,
        b0_ref,
        b1_ref,
        b2_ref,
        c_ref,
        obc_ref,
        ob_ref,
        acc_ref,
        part_ref,
        got_ref,
        left_sem,
        send_sem,
        recv_sem,
        send2_sem,
        recv2_sem,
    ) = refs
    gz, tx, ty = place()
    load_left = pltpu.make_async_copy(left_hbm, left_ref, left_sem)
    load_left.start()

    halo_ref[...] = jnp.zeros(halo_ref.shape, f32)
    if comm:
        offsets = [(dx, dy, dz) for dx in (-1, 0, 1) for dy in (-1, 0, 1) for dz in (-1, 0, 1)]
        offsets = [o for o in offsets if o != (0, 0, 0)]

        def neighbour(dx, dy, dz):
            at = ((tx + dx + 8) % 8) * 8 + (ty + dy + 8) % 8
            return {"gz": (gz + dz + 4) % 4, "xy": at}

        tile = tx * 8 + ty
        zpos = gz * 4 + tile % 4
        column = tile // 4

        def along_z(step):
            other = (zpos + step) % 16
            return {"gz": other // 4, "xy": column * 4 + other % 4}

        def along_plane(step):
            return {"gz": gz, "xy": ((column + step) % 16) * 4 + tile % 4}

        barrier = pltpu.get_barrier_semaphore()
        partners = [neighbour(*o) for o in offsets]
        partners += [f(step) for f in (along_z, along_plane) for step in range(1, 16)]
        for device in partners:
            pl.semaphore_signal(barrier, inc=1, device_id=device, device_id_type=pl.DeviceIdType.MESH)

    codes = codes_ref[...]
    base = jnp.zeros((8, 128), f32)
    for level in range(4):
        base = jnp.where(codes == level, table_ref[level], base)
    site = sites_ref[...]
    lz = (site >> 14) - gz * 4
    lx = ((site >> 7) & 127) - tx * 16
    ly = (site & 127) - ty * 16
    inside = (lz >= 0) & (lz < 4) & (lx >= 0) & (lx < 16) & (ly >= 0) & (ly < 16)
    row = jnp.where(inside, lz * 2 + (lx >> 3), -1)
    col = (lx & 7) * 16 + ly
    pieces = split3(strength_ref[...])
    lhs, rhs = [], []
    for k in range(32):
        hit = jnp.broadcast_to(row[k : k + 1], (8, 128)) == iota((8, 128), 0)
        lhs.append(
            rows(
                [jnp.where(hit, jnp.broadcast_to(p[k : k + 1].astype(f32), (8, 128)), 0.0) for p in pieces]
                + [jnp.zeros((8, 128), f32)]
            ).astype(bf16)
        )
        at = jnp.broadcast_to(col[k : k + 1], (128, 128)) == iota((128, 128), 0)
        rhs.append(jnp.where(at, 1.0, 0.0).astype(bf16))
    added = lax.dot_general(lanes_of(lhs), lanes_of(rhs), NT, preferred_element_type=f32)
    onsite = base + (added[0:8] + added[8:16] + added[16:24])
    for z in range(4):
        for h in range(2):
            halo_ref[4, h, 8 + z : 9 + z] = onsite[2 * z + h : 2 * z + h + 1]

    spread = jnp.where(iota((8, 128), 1) >> 4 == iota((8, 128), 0), 1.0, 0.0)
    mass_raw = mass_ref[...]
    mass = 0.5 * (mass_raw + mass_raw.T)
    mats = [mass]
    for d in range(3):
        mats += [hop_ref[d].T, hop_ref[d]]
    wide = jnp.dot(rows(mats) * 0.4, spread, precision=highest, preferred_element_type=f32)
    same_r = (iota((16, 128), 1) & 15) == iota((16, 128), 0)
    full = []
    for k in range(7):
        blocks = []
        for b in range(8):
            row = wide[8 * k + b : 8 * k + b + 1]
            blocks.append(jnp.where(same_r, jnp.broadcast_to(row, (16, 128)), 0.0))
        full.append(split2(rows(blocks)))
    for slot, k in enumerate((0, 1, 2, 5, 6)):
        both = lanes_of(full[k])
        wm_ref[256 * slot : 256 * slot + 128] = both
        wm_ref[256 * slot + 128 : 256 * slot + 256] = both
    for part in range(2):
        both = lanes_of([full[3][part], full[4][part]])
        wy_ref[256 * part : 256 * part + 128] = both
        wy_ref[256 * part + 128 : 256 * part + 256] = both
    w0_ref[0:128] = lanes_of(full[1])
    w0_ref[128:256] = -lanes_of(full[2])
    for part in range(2):
        wz_ref[128 * part : 128 * part + 128] = lanes_of(
            [full[6][part], full[6][part], -full[5][part], -full[5][part]]
        )

    x, y = rows_to_xy(iota((576, 128), 0) + 8)
    lane = iota((576, 128), 1)
    xg = (tx * 16 + x + 128) & 127
    yg = ty * 16 + y
    lane1 = iota((1, 128), 1) & 15
    seeds = jnp.zeros((1, 128), i32)
    for r in range(16):
        seeds = jnp.where(lane1 == r, seed_ref[r], seeds)
    hb_ref[...] = ((xg * 128 + yg) * 8 + (lane >> 4)) * MULT + seeds
    mk_ref[...] = jnp.where((yg >= 0) & (yg < 128), 1.0, 0.0)

    def sign_plane(p, carry):
        zg = (gz * 4 + p + 12) & 15
        word = hb_ref[...] + zg * wrap32(128 * 128 * 8 * MULT)
        word = word ^ lax.shift_right_logical(word, jnp.full(word.shape, 15, i32))
        word = word * -2048144789
        word = word ^ lax.shift_right_logical(word, jnp.full(word.shape, 13, i32))
        word = word * -1028477387
        mk = mk_ref[...]
        sb_ref[p] = jnp.where(word < 0, -mk, mk).astype(bf16)
        return carry

    lax.fori_loop(0, 12, sign_plane, 0)

    fs = (f0_ref, f1_ref, f2_ref)
    as_ = (a0_ref, a1_ref, a2_ref)
    bs = (b0_ref, b1_ref, b2_ref)

    def keep(level, p, out, lo, hi, own):
        hi_f = out.astype(bf16).astype(f32)
        both = lanes_of([hi_f, out - hi_f])
        as_[level][p, lo:hi] = both.astype(bf16)
        bs[level][p, lo - 16 : hi] = rows([both[:8], both, both[:8]]).astype(bf16)
        if own:
            c_ref[level, p - 3] = own_rows(both, lo).astype(bf16)

    def start(planes, lo, hi, own):
        size = hi - lo
        lhs = rows([lanes_of([sb_ref[p, lo + 16 : hi + 16], sb_ref[p, lo - 32 : hi - 32]]) for p in planes])
        prod = jnp.dot(lhs, w0_ref[...], preferred_element_type=f32)
        prod = (prod[:, :128] + prod[:, 128:]) * 2.5
        for k, p in enumerate(planes):
            out = prod[k * size : k * size + size]
            f0_ref[p, lo:hi] = out
            keep(0, p, out, lo, hi, own)

    each_group(3, start)

    if comm:
        pl.semaphore_wait(barrier, len(partners))
        mine = halo_ref.at[4, :, pl.ds(8, 8)]
        sends = []
        for k, (dx, dy, dz) in enumerate(offsets):
            send = pltpu.make_async_remote_copy(
                src_ref=mine,
                dst_ref=halo_ref.at[(1 - dx) * 3 + 1 - dy, :, pl.ds(8 * (1 - dz), 8)],
                send_sem=send_sem.at[k],
                recv_sem=recv_sem.at[k],
                device_id=neighbour(dx, dy, dz),
                device_id_type=pl.DeviceIdType.MESH,
            )
            send.start()
            sends.append(send)

    def hop(n, planes, lo, hi):
        a_ref, b_ref = as_[n], bs[n]
        lhs = [
            lanes_of(
                [
                    a_ref[p, lo:hi],
                    b_ref[p, lo + 16 : hi + 16],
                    b_ref[p, lo - 32 : hi - 32],
                    a_ref[p + 1, lo:hi],
                    a_ref[p - 1, lo:hi],
                ]
            )
            for p in planes
        ]
        main = jnp.dot(rows(lhs), wm_ref[...], preferred_element_type=f32)
        size = hi - lo
        first = 0 if (lo, hi) == LOHI[1] else 16
        ylhs = rows([a_ref[p, lo - first : lo - first + size + 16] for p in planes])
        yy = jnp.dot(lanes_of([ylhs, ylhs]), wy_ref[...], preferred_element_type=f32)
        total = len(planes) * (size + 16)
        yp = pltpu.roll(yy[:, :128], total - 1, 0)
        ym = pltpu.roll(yy[:, 128:], 1, 0)
        outs = []
        for k in range(len(planes)):
            r, s = k * size, k * (size + 16) + first
            outs.append(main[r : r + size, :128] + main[r : r + size, 128:] + yp[s : s + size] + ym[s : s + size])
        return outs

    def first_hop(planes, lo, hi, own):
        for p, out in zip(planes, hop(0, planes, lo, hi)):
            f1_ref[p, lo:hi] = out

    each_group(2, first_hop)

    if comm:
        for send in sends:
            send.wait()
    else:
        halo_ref[...] = halo_in[...]
    obc_ref[...] = jnp.zeros(obc_ref.shape, f32)
    for dx, h, lo, hi in ((0, 0, 96, 304), (0, 1, 288, 496), (-1, 1, 64, 112), (1, 0, 480, 544)):
        xr, yr = rows_to_xy(iota((hi - lo, 128), 0) + lo)
        xr = xr - 16 * dx - 8 * h
        ok = (xr >= 0) & (xr < 8)
        lane = iota((hi - lo, 128), 1)
        sels, vals = [], []
        for dy in (-1, 0, 1):
            yy = yr - 16 * dy
            hit = ok & (yy >= 0) & (yy < 16) & (xr * 16 + yy == lane)
            sel = jnp.where(hit, 1.0, 0.0).astype(bf16)
            for piece in split3(halo_ref[(dx + 1) * 3 + dy + 1, h]):
                sels.append(sel)
                vals.append(piece)
        obc_ref[lo - 64 : hi - 64] += lax.dot_general(
            lanes_of(sels), lanes_of(vals), NT, preferred_element_type=f32
        )
    for p in range(1, 11):
        col = (p // 4) * 8 + p % 4
        ob_ref[p - 1] = jnp.broadcast_to(obc_ref[:, col : col + 1] * 0.4, (480, 128))

    def site_term(n, p, lo, hi):
        return ob_ref[p - 1, lo - 64 : hi - 64] * fs[n][p, lo:hi]

    def first_rest(planes, lo, hi, own):
        mask = mk_ref[lo - 8 : hi - 8] * 0.5
        for p in planes:
            out = (f1_ref[p, lo:hi] + site_term(0, p, lo, hi)) * mask
            f1_ref[p, lo:hi] = out
            keep(1, p, out, lo, hi, own)

    each_group(2, first_rest)

    def step(n, planes, lo, hi, own):
        mask = mk_ref[lo - 8 : hi - 8]
        for p, out in zip(planes, hop(n, planes, lo, hi)):
            out = (out + site_term(n, p, lo, hi)) * mask - fs[n - 1][p, lo:hi]
            if n == 1:
                f2_ref[p, lo:hi] = out
                keep(2, p, out, lo, hi, own)
            else:
                v = own_rows(out, lo)
                hi_f = v.astype(bf16).astype(f32)
                c_ref[3, p - 3] = lanes_of([hi_f, v - hi_f]).astype(bf16)
                f0_ref[p, 0:256] = v

    each_group(1, functools.partial(step, 1))
    each_group(0, functools.partial(step, 2))

    acc_ref[...] = jnp.zeros(acc_ref.shape, f32)
    load_left.wait()

    def plane_moments(z, carry):
        us = []
        for n in range(4):
            rhs = lanes_of([c_ref[n, z + 2], c_ref[n, z]])
            u = lax.dot_general(wz_ref[...], rhs, NT, preferred_element_type=f32)
            us.append(u[:128] + u[128:])
        for h in range(2):
            for m in range(3):
                lv = left_ref[m, pl.ds(2 * z + h, 128, stride=8), :]
                for n in range(4):
                    prod = lv * us[n][:, 128 * h : 128 * h + 128]
                    tot = prod[0:16]
                    for o in range(1, 8):
                        tot = tot + prod[16 * o : 16 * o + 16]
                    acc_ref[m * 4 + n] += tot
        return carry

    lax.fori_loop(0, 4, plane_moments, 0)
    lanes = iota((8, 128), 1)
    part = jnp.zeros((8, 128), f32)
    for k in range(12):
        tot = jnp.sum(acc_ref[k], axis=1, keepdims=True)
        part = jnp.where(lanes == k, tot[0:8], part)
        part = jnp.where(lanes == k + 16, tot[8:16], part)
    part = part * (2.5 / math.sqrt(8 * 262144))
    part_ref[0] = part

    def send_part(stage, target):
        copies = []
        for step in range(1, 16):
            copy = pltpu.make_async_remote_copy(
                src_ref=part_ref.at[stage],
                dst_ref=got_ref.at[stage, step - 1],
                send_sem=send2_sem.at[stage, step - 1],
                recv_sem=recv2_sem.at[stage, step - 1],
                device_id=target(step),
                device_id_type=pl.DeviceIdType.MESH,
            )
            copy.start()
            copies.append(copy)
        return copies

    def add_parts(stage, copies, total):
        for copy in copies:
            copy.wait()
        for step in range(1, 16):
            total = total + got_ref[stage, step - 1]
        return total

    if comm:
        copies = send_part(0, along_z)

    def plane_out(z, carry):
        last = f0_ref[z + 4, 0:256].T
        prev = own_rows(f2_ref[z + 4, 80:512], 80).T
        for h in range(2):
            last_ref[pl.ds(2 * z + h, 128, stride=8), :] = last[:, 128 * h : 128 * h + 128]
            prev_ref[pl.ds(2 * z + h, 128, stride=8), :] = prev[:, 128 * h : 128 * h + 128]
        return carry

    lax.fori_loop(0, 4, plane_out, 0)

    if comm:
        part = add_parts(0, copies, part)
        part_ref[1] = part
        part = add_parts(1, send_part(1, along_plane), part)
    flat = rows([part, jnp.zeros((120, 128), f32)]).T
    for m in range(3):
        moments_ref[m, :, 0:8] = flat[4 * m : 4 * m + 4, 0:8]
        moments_ref[m, :, 8:16] = flat[16 + 4 * m : 20 + 4 * m, 0:8]


def whole(place, comm, seeds, hoppings, mass_raw, codes, table, sites, strength, left, *halo):
    vm = pl.BlockSpec(memory_space=pltpu.VMEM)
    sm = pl.BlockSpec(memory_space=pltpu.SMEM)
    plane = lambda kind, lanes: pltpu.VMEM((12, NR, lanes), kind)
    dma = pltpu.SemaphoreType.DMA
    extra = {"collective_id": 0, "has_side_effects": True} if comm else {}
    return pl.pallas_call(
        functools.partial(kernel, place, comm),
        out_shape=(
            jax.ShapeDtypeStruct((3, 4, 16), f32),
            jax.ShapeDtypeStruct((1024, 128), f32),
            jax.ShapeDtypeStruct((1024, 128), f32),
        ),
        in_specs=[sm, vm, vm, vm, sm, vm, vm, pl.BlockSpec(memory_space=pl.ANY)] + [vm] * len(halo),
        out_specs=(vm, vm, vm),
        scratch_shapes=[
            pltpu.VMEM((9, 2, 32, 128), f32),
            pltpu.VMEM((3, 1024, 128), f32),
            pltpu.VMEM((1280, 256), bf16),
            pltpu.VMEM((512, 256), bf16),
            pltpu.VMEM((256, 256), bf16),
            pltpu.VMEM((256, 512), bf16),
            pltpu.VMEM((576, 128), i32),
            pltpu.VMEM((576, 128), f32),
            pltpu.VMEM((12, 576, 128), bf16),
            plane(f32, 128),
            plane(f32, 128),
            plane(f32, 128),
            plane(bf16, 256),
            plane(bf16, 256),
            plane(bf16, 256),
            plane(bf16, 256),
            plane(bf16, 256),
            plane(bf16, 256),
            pltpu.VMEM((4, 6, 256, 256), bf16),
            pltpu.VMEM((480, 32), f32),
            pltpu.VMEM((10, 480, 128), f32),
            pltpu.VMEM((12, 16, 128), f32),
            pltpu.VMEM((2, 8, 128), f32),
            pltpu.VMEM((2, 15, 8, 128), f32),
            dma,
            dma((26,)),
            dma((26,)),
            dma((2, 15)),
            dma((2, 15)),
        ],
        compiler_params=pltpu.CompilerParams(vmem_limit_bytes=60 * 1024 * 1024, **extra),
        name="chain",
    )(seeds, hoppings, mass_raw, codes, table, sites, strength, left, *halo)


def where_am_i():
    tile = lax.axis_index("xy")
    return lax.axis_index("gz"), tile // 8, tile % 8


def per_device(
    left_vectors,
    sign_seeds,
    level_codes,
    level_table,
    disorder_sites,
    disorder_strength,
    hoppings,
    mass_raw,
):
    moments, prev, last = whole(
        where_am_i,
        True,
        sign_seeds,
        hoppings,
        mass_raw,
        level_codes.reshape(8, 128),
        level_table,
        disorder_sites.reshape(32, 128),
        disorder_strength.reshape(32, 128),
        left_vectors.reshape(3, 1024, 128),
    )
    shape = left_vectors.shape[1:]
    return moments, prev.reshape(shape), last.reshape(shape)


def solution(mesh):
    in_specs = (
        P(None, None, None, "gz", "xy", None),
        P(),
        P("gz", "xy", None),
        P(),
        P(),
        P(),
        P(),
        P(),
    )
    out_specs = (P(), P(None, None, "gz", "xy", None), P(None, None, "gz", "xy", None))
    return jax.shard_map(
        per_device, mesh=mesh, in_specs=in_specs, out_specs=out_specs, check_vma=False
    )
```

```python
import functools
import math

import jax
import jax.numpy as jnp
from jax import lax
from jax.experimental import pallas as pl
from jax.experimental.pallas import tpu as pltpu
from jax.sharding import PartitionSpec as P

f32, bf16, i32 = jnp.float32, jnp.bfloat16, jnp.int32

PITCH = 24
NR = 608
LOHI = {0: (112, 496), 1: (80, 512), 2: (64, 544), 3: (32, 560)}
MULT = 668265261
NT = (((1,), (1,)), ((), ()))
highest = lax.Precision.HIGHEST


def split2(v):
    hi = v.astype(bf16)
    lo = (v - hi.astype(f32)).astype(bf16)
    return hi, lo


def split3(v):
    hi = v.astype(bf16)
    rest = v - hi.astype(f32)
    mid = rest.astype(bf16)
    lo = (rest - mid.astype(f32)).astype(bf16)
    return hi, mid, lo


def iota(shape, dim):
    return lax.broadcasted_iota(i32, shape, dim)


def rows_to_xy(rows):
    i = rows - 12
    q = lax.shift_right_arithmetic(i * 2731, jnp.full(i.shape, 16, i32))
    return q - 4, i - q * 24 - 4


def own_rows(block, lo):
    return jnp.concatenate(
        [block[112 + 24 * x - lo : 112 + 24 * x - lo + 16] for x in range(16)], axis=0
    )


def wrap32(value):
    value &= 0xFFFFFFFF
    return value - (1 << 32) if value >= (1 << 31) else value


def rows(parts):
    return jnp.concatenate(parts, axis=0)


def lanes_of(parts):
    return jnp.concatenate(parts, axis=1)


MESH = pl.DeviceIdType.MESH
SEGMENTS = ((0, 0, 96, 304), (0, 1, 288, 496), (-1, 1, 64, 112), (1, 0, 480, 544))


def kernel(
    place,
    comm,
    seed_hbm,
    hop_hbm,
    mass_hbm,
    codes_hbm,
    table_hbm,
    sites_hbm,
    strength_hbm,
    left_hbm,
    *refs,
):
    if not comm:
        (halo_in, a1_in, a2_in, c_in), refs = refs[:4], refs[4:]
    (
        moments_ref,
        prev_ref,
        last_ref,
        seed_ref,
        hop_ref,
        mass_ref,
        codes_ref,
        table_ref,
        sites_ref,
        strength_ref,
        left_ref,
        halo_ref,
        wm_ref,
        wy_ref,
        w0_ref,
        wz_ref,
        hb_ref,
        mk_ref,
        sb_ref,
        f0_ref,
        f1_ref,
        f2_ref,
        a0_ref,
        a1_ref,
        a2_ref,
        b0_ref,
        b1_ref,
        b2_ref,
        c_ref,
        sel_ref,
        obc_ref,
        ob_ref,
        acc_ref,
        part_ref,
        got_ref,
        load_sem,
        send_sem,
        recv_sem,
        pair_send_sem,
        pair_recv_sem,
        send2_sem,
        recv2_sem,
    ) = refs
    gz, tx, ty = place()
    odd = gz % 2 == 1
    flip = gz % 2 * 2 - 1

    def z_of(p):
        return (3 * (1 - gz % 2)) + flip * (p - 1)

    if comm:
        near = [(dx, dy) for dx in (-1, 0, 1) for dy in (-1, 0, 1) if (dx, dy) != (0, 0)]
        outer = (gz + flip + 4) % 4
        inner = (gz - flip + 4) % 4
        tile = tx * 8 + ty
        zpos = gz * 4 + tile % 4
        column = tile // 4

        def neighbour(dx, dy, z):
            return {"gz": z, "xy": ((tx + dx + 8) % 8) * 8 + (ty + dy + 8) % 8}

        def along_z(step):
            other = (zpos + step) % 16
            return {"gz": other // 4, "xy": column * 4 + other % 4}

        def along_plane(step):
            return {"gz": gz, "xy": ((column + step) % 16) * 4 + tile % 4}

        barrier = pltpu.get_barrier_semaphore()
        partners = [neighbour(dx, dy, outer) for dx, dy in near]
        partners += [neighbour(dx, dy, gz) for dx, dy in near]
        partners += [f(step) for f in (along_z, along_plane) for step in range(1, 16)]
        for device in partners:
            pl.semaphore_signal(barrier, inc=1, device_id=device, device_id_type=MESH)

    loads = []
    for k, (src, dst) in enumerate(
        (
            (sites_hbm, sites_ref),
            (strength_hbm, strength_ref),
            (codes_hbm, codes_ref),
            (table_hbm, table_ref),
            (hop_hbm, hop_ref),
            (mass_hbm, mass_ref),
            (seed_hbm, seed_ref),
            (left_hbm, left_ref),
        )
    ):
        loads.append(pltpu.make_async_copy(src, dst, load_sem.at[k]))
        loads[-1].start()

    for load in loads[:4]:
        load.wait()
    codes = codes_ref[...]
    base = jnp.zeros((8, 128), f32)
    for level in range(4):
        base = jnp.where(codes == level, table_ref[level], base)
    site = sites_ref[...]
    lz = (site >> 14) - gz * 4
    lx = ((site >> 7) & 127) - tx * 16
    ly = (site & 127) - ty * 16
    inside = (lz >= 0) & (lz < 4) & (lx >= 0) & (lx < 16) & (ly >= 0) & (ly < 16)
    row = jnp.where(inside, lz * 2 + (lx >> 3), -1)
    col = (lx & 7) * 16 + ly
    pieces = split3(strength_ref[...])
    lhs, rhs = [], []
    for k in range(32):
        hit = jnp.broadcast_to(row[k : k + 1], (8, 128)) == iota((8, 128), 0)
        lhs.append(
            rows(
                [jnp.where(hit, jnp.broadcast_to(p[k : k + 1].astype(f32), (8, 128)), 0.0) for p in pieces]
                + [jnp.zeros((8, 128), f32)]
            ).astype(bf16)
        )
        at = jnp.broadcast_to(col[k : k + 1], (128, 128)) == iota((128, 128), 0)
        rhs.append(jnp.where(at, 1.0, 0.0).astype(bf16))
    added = lax.dot_general(lanes_of(lhs), lanes_of(rhs), NT, preferred_element_type=f32)
    onsite = base + (added[0:8] + added[8:16] + added[16:24])
    for h in range(2):
        up = [onsite[2 * z + h : 2 * z + h + 1] for z in range(4)]
        block = jnp.where(odd, rows(up), rows(up[::-1]))
        halo_ref[0, 4, h] = rows([block, jnp.zeros((4, 128), f32)])

    if comm:
        pl.semaphore_wait(barrier, len(partners))
        near_sends, far_sends = [], []
        for k, (dx, dy, far) in enumerate(
            [(dx, dy, True) for dx, dy in near] + [(0, 0, True)] + [(dx, dy, False) for dx, dy in near]
        ):
            send = pltpu.make_async_remote_copy(
                src_ref=halo_ref.at[0, 4],
                dst_ref=halo_ref.at[int(far), (1 - dx) * 3 + 1 - dy],
                send_sem=send_sem.at[k],
                recv_sem=recv_sem.at[k],
                device_id=neighbour(dx, dy, outer if far else gz),
                device_id_type=MESH,
            )
            send.start()
            (far_sends if far else near_sends).append(send)

    for load in loads[4:7]:
        load.wait()
    spread = jnp.where(iota((8, 128), 1) >> 4 == iota((8, 128), 0), 1.0, 0.0)
    mass_raw = mass_ref[...]
    mats = [0.5 * (mass_raw + mass_raw.T)]
    for d in range(3):
        mats += [hop_ref[d].T, hop_ref[d]]
    wide = jnp.dot(rows(mats) * 0.4, spread, precision=highest, preferred_element_type=f32)
    wide = [wide[8 * k : 8 * k + 8] for k in range(7)]
    same_r = (iota((16, 128), 1) & 15) == iota((16, 128), 0)

    def matrix(narrow):
        blocks = [jnp.where(same_r, jnp.broadcast_to(narrow[b : b + 1], (16, 128)), 0.0) for b in range(8)]
        return split2(rows(blocks))

    w_mass, w_xp, w_xm, w_yp, w_ym = [matrix(w) for w in wide[:5]]
    w_next = matrix(jnp.where(odd, wide[5], wide[6]))
    w_before = matrix(jnp.where(odd, wide[6], wide[5]))
    v_next = matrix(jnp.where(odd, wide[6], -wide[5]))
    v_before = matrix(jnp.where(odd, -wide[5], wide[6]))
    for slot, pair in enumerate((w_mass, w_xp, w_xm, w_next, w_before)):
        both = lanes_of(pair)
        wm_ref[256 * slot : 256 * slot + 128] = both
        wm_ref[256 * slot + 128 : 256 * slot + 256] = both
    for part in range(2):
        both = lanes_of([w_yp[part], w_ym[part]])
        wy_ref[256 * part : 256 * part + 128] = both
        wy_ref[256 * part + 128 : 256 * part + 256] = both
        wz_ref[128 * part : 128 * part + 128] = lanes_of([v_next[part]] * 2 + [v_before[part]] * 2)
    w0_ref[0:128] = lanes_of(w_xp)
    w0_ref[128:256] = -lanes_of(w_xm)

    x, y = rows_to_xy(iota((576, 128), 0) + 8)
    lane = iota((576, 128), 1)
    xg = (tx * 16 + x + 128) & 127
    yg = ty * 16 + y
    lane1 = iota((1, 128), 1) & 15
    seeds = jnp.zeros((1, 128), i32)
    for r in range(16):
        seeds = jnp.where(lane1 == r, seed_ref[r], seeds)
    hb_ref[...] = ((xg * 128 + yg) * 8 + (lane >> 4)) * MULT + seeds
    mk_ref[...] = jnp.where((yg >= 0) & (yg < 128), 1.0, 0.0)

    def sign_plane(p, carry):
        zg = (gz * 4 + z_of(p) + 16) & 15
        word = hb_ref[...] + zg * wrap32(128 * 128 * 8 * MULT)
        word = word ^ lax.shift_right_logical(word, jnp.full(word.shape, 15, i32))
        word = word * -2048144789
        word = word ^ lax.shift_right_logical(word, jnp.full(word.shape, 13, i32))
        word = word * -1028477387
        mk = mk_ref[...]
        sb_ref[p] = jnp.where(word < 0, -mk, mk).astype(bf16)
        return carry

    lax.fori_loop(0, 9, sign_plane, 0)

    at = 0
    for dx, h, lo, hi in SEGMENTS:
        xr, yr = rows_to_xy(iota((hi - lo, 128), 0) + lo)
        xr = xr - 16 * dx - 8 * h
        ok = (xr >= 0) & (xr < 8)
        lane = iota((hi - lo, 128), 1)
        sels = []
        for dy in (-1, 0, 1):
            yy = yr - 16 * dy
            hit = ok & (yy >= 0) & (yy < 16) & (xr * 16 + yy == lane)
            sels.append(jnp.where(hit, 1.0, 0.0).astype(bf16))
        sel_ref[at : at + hi - lo] = lanes_of(sels)
        at += hi - lo

    fs = (f0_ref, f1_ref, f2_ref)
    as_ = (a0_ref, a1_ref, a2_ref)
    bs = (b0_ref, b1_ref, b2_ref)

    def keep(level, p, out, lo, hi):
        hi_f = out.astype(bf16).astype(f32)
        both = lanes_of([hi_f, out - hi_f])
        as_[level][p, lo:hi] = both.astype(bf16)
        bs[level][p, lo - 16 : hi] = rows([both[:8], both, both[:8]]).astype(bf16)
        if p <= 5:
            c_ref[level, p] = own_rows(both, lo).astype(bf16)

    def start(planes):
        lhs = []
        for p, radius in planes:
            lo, hi = LOHI[radius]
            lhs.append(lanes_of([sb_ref[p, lo + 16 : hi + 16], sb_ref[p, lo - 32 : hi - 32]]))
        prod = jnp.dot(rows(lhs), w0_ref[...], preferred_element_type=f32)
        prod = (prod[:, :128] + prod[:, 128:]) * 2.5
        at = 0
        for p, radius in planes:
            lo, hi = LOHI[radius]
            out = prod[at : at + hi - lo]
            at += hi - lo
            f0_ref[p, lo:hi] = out
            keep(0, p, out, lo, hi)

    start(((0, 2), (1, 3), (2, 3)))
    start(((3, 3), (4, 3), (5, 3)))
    start(((6, 2), (7, 1), (8, 0)))

    def hop(n, planes):
        a_ref, b_ref = as_[n], bs[n]
        lhs, ylhs = [], []
        for p, radius in planes:
            lo, hi = LOHI[radius]
            lhs.append(
                lanes_of(
                    [
                        a_ref[p, lo:hi],
                        b_ref[p, lo + 16 : hi + 16],
                        b_ref[p, lo - 32 : hi - 32],
                        a_ref[p + 1, lo:hi],
                        a_ref[p - 1, lo:hi],
                    ]
                )
            )
            first = 0 if radius == 1 else 16
            ylhs.append(a_ref[p, lo - first : hi + 16 - first])
        main = jnp.dot(rows(lhs), wm_ref[...], preferred_element_type=f32)
        ylhs = rows(ylhs)
        yy = jnp.dot(lanes_of([ylhs, ylhs]), wy_ref[...], preferred_element_type=f32)
        yp = pltpu.roll(yy[:, :128], yy.shape[0] - 1, 0)
        ym = pltpu.roll(yy[:, 128:], 1, 0)
        outs, r, s = [], 0, 0
        for p, radius in planes:
            lo, hi = LOHI[radius]
            first = 0 if radius == 1 else 16
            size, t = hi - lo, s + first
            outs.append(main[r : r + size, :128] + main[r : r + size, 128:] + yp[t : t + size] + ym[t : t + size])
            r += size
            s += size + 16
        return outs

    def first_hop(planes):
        for (p, radius), out in zip(planes, hop(0, planes)):
            lo, hi = LOHI[radius]
            f1_ref[p, lo:hi] = out

    first_hop(((1, 2), (2, 2), (3, 2)))
    first_hop(((4, 2), (5, 2), (6, 1), (7, 0)))

    def energies(far, planes):
        obc_ref[...] = jnp.zeros(obc_ref.shape, f32)
        at = 0
        for dx, h, lo, hi in SEGMENTS:
            sels, vals = [], []
            for dy in (-1, 0, 1):
                sel = sel_ref[at : at + hi - lo, 128 * (dy + 1) : 128 * (dy + 2)]
                block = halo_ref[far, (dx + 1) * 3 + dy + 1, h]
                for piece in split3(rows([block, jnp.zeros((8, 128), f32)])):
                    sels.append(sel)
                    vals.append(piece)
            at += hi - lo
            obc_ref[lo - 64 : hi - 64] += lax.dot_general(
                lanes_of(sels), lanes_of(vals), NT, preferred_element_type=f32
            )
        for p, col in planes:
            ob_ref[p] = jnp.broadcast_to(obc_ref[:, col : col + 1] * 0.4, (480, 128))

    def site_term(n, p, lo, hi):
        return ob_ref[p, lo - 64 : hi - 64] * fs[n][p, lo:hi]

    def first_rest(planes):
        for p, radius in planes:
            lo, hi = LOHI[radius]
            out = (f1_ref[p, lo:hi] + site_term(0, p, lo, hi)) * (mk_ref[lo - 8 : hi - 8] * 0.5)
            f1_ref[p, lo:hi] = out
            keep(1, p, out, lo, hi)

    def step(n, planes):
        for (p, radius), out in zip(planes, hop(n, planes)):
            lo, hi = LOHI[radius]
            out = (out + site_term(n, p, lo, hi)) * mk_ref[lo - 8 : hi - 8] - fs[n - 1][p, lo:hi]
            if n == 1:
                f2_ref[p, lo:hi] = out
                keep(2, p, out, lo, hi)
            else:
                v = own_rows(out, lo)
                hi_f = v.astype(bf16).astype(f32)
                c_ref[3, p] = lanes_of([hi_f, v - hi_f]).astype(bf16)
                f0_ref[p, 0:256] = v

    pair_sends = []

    def to_pair(level):
        if not comm:
            if level < 3:
                as_[level][0] = (a1_in, a2_in)[level - 1][...]
            c_ref[level, 0] = c_in[level - 1]
            return
        moves = [(c_ref.at[level, 1], c_ref.at[level, 0])]
        if level < 3:
            lo, hi = LOHI[2 - level]
            a_ref = as_[level]
            moves.append((a_ref.at[1, pl.ds(lo, hi - lo)], a_ref.at[0, pl.ds(lo, hi - lo)]))
        for k, (src, dst) in enumerate(moves):
            pair_sends.append(
                pltpu.make_async_remote_copy(
                    src_ref=src,
                    dst_ref=dst,
                    send_sem=pair_send_sem.at[level - 1, k],
                    recv_sem=pair_recv_sem.at[level - 1, k],
                    device_id={"gz": inner, "xy": tile},
                    device_id_type=MESH,
                )
            )
            pair_sends[-1].start()

    def from_pair():
        for send in pair_sends:
            send.wait()
        del pair_sends[:]

    acc_ref[...] = jnp.zeros(acc_ref.shape, f32)

    def moments_of(orders):
        def one(p, carry):
            us = []
            for n in orders:
                rhs = lanes_of([c_ref[n, p + 1], c_ref[n, p - 1]])
                u = lax.dot_general(wz_ref[...], rhs, NT, preferred_element_type=f32)
                us.append(u[:128] + u[128:])
            for h in range(2):
                for m in range(3):
                    lv = left_ref[m, pl.ds(2 * z_of(p) + h, 128, stride=8), :]
                    for n, u in zip(orders, us):
                        prod = lv * u[:, 128 * h : 128 * h + 128]
                        tot = prod[0:16]
                        for o in range(1, 8):
                            tot = tot + prod[16 * o : 16 * o + 16]
                        acc_ref[m * 4 + n] += tot
            return carry

        lax.fori_loop(1, 5, one, 0)

    if comm:
        for send in near_sends:
            send.wait()
    else:
        halo_ref[...] = halo_in[...]
    energies(0, [(p, p - 1) for p in range(1, 5)])
    first_rest(((1, 2),))
    to_pair(1)
    first_rest(((2, 2), (3, 2), (4, 2)))
    loads[7].wait()
    moments_of((0,))
    from_pair()
    step(1, ((1, 1), (2, 1), (3, 1)))
    to_pair(2)
    if comm:
        for send in far_sends:
            send.wait()
    energies(1, [(p, 8 - p) for p in range(5, 8)])
    first_rest(((5, 2), (6, 1), (7, 0)))
    step(1, ((4, 1), (5, 1), (6, 0)))
    from_pair()
    step(2, ((1, 0), (2, 0)))
    to_pair(3)
    step(2, ((3, 0), (4, 0), (5, 0)))
    from_pair()
    moments_of((1, 2, 3))
    lanes = iota((8, 128), 1)
    part = jnp.zeros((8, 128), f32)
    for k in range(12):
        tot = jnp.sum(acc_ref[k], axis=1, keepdims=True)
        part = jnp.where(lanes == k, tot[0:8], part)
        part = jnp.where(lanes == k + 16, tot[8:16], part)
    part = part * (2.5 / math.sqrt(8 * 262144))
    part_ref[0] = part

    def send_part(stage, target):
        copies = []
        for step in range(1, 16):
            copy = pltpu.make_async_remote_copy(
                src_ref=part_ref.at[stage],
                dst_ref=got_ref.at[stage, step - 1],
                send_sem=send2_sem.at[stage, step - 1],
                recv_sem=recv2_sem.at[stage, step - 1],
                device_id=target(step),
                device_id_type=MESH,
            )
            copy.start()
            copies.append(copy)
        return copies

    def add_parts(stage, copies, total):
        for copy in copies:
            copy.wait()
        for step in range(1, 16):
            total = total + got_ref[stage, step - 1]
        return total

    if comm:
        copies = send_part(0, along_z)

    def plane_out(p, carry):
        last = f0_ref[p, 0:256].T
        prev = own_rows(f2_ref[p, 80:512], 80).T
        for h in range(2):
            place_of = pl.ds(2 * z_of(p) + h, 128, stride=8)
            last_ref[place_of, :] = last[:, 128 * h : 128 * h + 128]
            prev_ref[place_of, :] = prev[:, 128 * h : 128 * h + 128]
        return carry

    lax.fori_loop(1, 5, plane_out, 0)

    if comm:
        part = add_parts(0, copies, part)
        part_ref[1] = part
        part = add_parts(1, send_part(1, along_plane), part)
    flat = rows([part, jnp.zeros((120, 128), f32)]).T
    for m in range(3):
        moments_ref[m, :, 0:8] = flat[4 * m : 4 * m + 4, 0:8]
        moments_ref[m, :, 8:16] = flat[16 + 4 * m : 20 + 4 * m, 0:8]


def whole(place, comm, *operands):
    hbm = pl.BlockSpec(memory_space=pltpu.HBM)
    vm = pl.BlockSpec(memory_space=pltpu.VMEM)
    plane = lambda kind, lanes: pltpu.VMEM((9, NR, lanes), kind)
    dma = pltpu.SemaphoreType.DMA
    extra = {"collective_id": 0, "has_side_effects": True} if comm else {}
    return pl.pallas_call(
        functools.partial(kernel, place, comm),
        out_shape=(
            jax.ShapeDtypeStruct((3, 4, 16), f32),
            jax.ShapeDtypeStruct((1024, 128), f32),
            jax.ShapeDtypeStruct((1024, 128), f32),
        ),
        in_specs=[hbm] * 8 + [vm] * (len(operands) - 8),
        out_specs=(vm, vm, vm),
        scratch_shapes=[
            pltpu.SMEM((16,), i32),
            pltpu.VMEM((3, 8, 8), f32),
            pltpu.VMEM((8, 8), f32),
            pltpu.VMEM((8, 128), i32),
            pltpu.SMEM((4,), f32),
            pltpu.VMEM((32, 128), i32),
            pltpu.VMEM((32, 128), f32),
            pltpu.VMEM((3, 1024, 128), f32),
            pltpu.VMEM((2, 9, 2, 8, 128), f32),
            pltpu.VMEM((1280, 256), bf16),
            pltpu.VMEM((512, 256), bf16),
            pltpu.VMEM((256, 256), bf16),
            pltpu.VMEM((256, 512), bf16),
            pltpu.VMEM((576, 128), i32),
            pltpu.VMEM((576, 128), f32),
            pltpu.VMEM((9, 576, 128), bf16),
            plane(f32, 128),
            plane(f32, 128),
            plane(f32, 128),
            plane(bf16, 256),
            plane(bf16, 256),
            plane(bf16, 256),
            plane(bf16, 256),
            plane(bf16, 256),
            plane(bf16, 256),
            pltpu.VMEM((4, 6, 256, 256), bf16),
            pltpu.VMEM((528, 384), bf16),
            pltpu.VMEM((480, 16), f32),
            pltpu.VMEM((8, 480, 128), f32),
            pltpu.VMEM((12, 16, 128), f32),
            pltpu.VMEM((2, 8, 128), f32),
            pltpu.VMEM((2, 15, 8, 128), f32),
            dma((8,)),
            dma((17,)),
            dma((17,)),
            dma((3, 2)),
            dma((3, 2)),
            dma((2, 15)),
            dma((2, 15)),
        ],
        compiler_params=pltpu.CompilerParams(vmem_limit_bytes=48 * 1024 * 1024, **extra),
        name="chain",
    )(*[pltpu.with_memory_space_constraint(a, pltpu.HBM) for a in operands[:8]], *operands[8:])


def copy_kernel(a_ref, b_ref, c_ref, a_out, b_out, c_out):
    a_out[...] = a_ref[...]
    b_out[...] = b_ref[...]
    c_out[...] = c_ref[...]


def copied(*arrays):
    spec = pl.BlockSpec(memory_space=pltpu.VMEM)
    return pl.pallas_call(
        copy_kernel,
        out_shape=[jax.ShapeDtypeStruct(a.shape, a.dtype) for a in arrays],
        in_specs=[spec] * 3,
        out_specs=[spec] * 3,
        compiler_params=pltpu.CompilerParams(vmem_limit_bytes=48 * 1024 * 1024),
        name="copied",
    )(*arrays)


def where_am_i():
    tile = lax.axis_index("xy")
    return lax.axis_index("gz"), tile // 8, tile % 8


def per_device(
    left_vectors,
    sign_seeds,
    level_codes,
    level_table,
    disorder_sites,
    disorder_strength,
    hoppings,
    mass_raw,
):
    moments, prev, last = whole(
        where_am_i,
        True,
        sign_seeds,
        hoppings,
        mass_raw,
        level_codes.reshape(8, 128),
        level_table,
        disorder_sites.reshape(32, 128),
        disorder_strength.reshape(32, 128),
        left_vectors.reshape(3, 1024, 128),
    )
    moments, prev, last = copied(moments, prev, last)
    shape = left_vectors.shape[1:]
    return moments, prev.reshape(shape), last.reshape(shape)


def solution(mesh):
    in_specs = (
        P(None, None, None, "gz", "xy", None),
        P(),
        P("gz", "xy", None),
        P(),
        P(),
        P(),
        P(),
        P(),
    )
    out_specs = (P(), P(None, None, "gz", "xy", None), P(None, None, "gz", "xy", None))
    return jax.shard_map(
        per_device, mesh=mesh, in_specs=in_specs, out_specs=out_specs, check_vma=False
    )
```

```python
import functools
import math

import jax
import jax.numpy as jnp
from jax import lax
from jax.experimental import pallas as pl
from jax.experimental.pallas import tpu as pltpu
from jax.sharding import PartitionSpec as P

f32, bf16, i32 = jnp.float32, jnp.bfloat16, jnp.int32

PITCH = 24
NR = 608
LOHI = {0: (112, 496), 1: (80, 512), 2: (64, 544), 3: (32, 560)}
MULT = 668265261
NT = (((1,), (1,)), ((), ()))
highest = lax.Precision.HIGHEST


def split2(v):
    hi = v.astype(bf16)
    lo = (v - hi.astype(f32)).astype(bf16)
    return hi, lo


def split3(v):
    hi = v.astype(bf16)
    rest = v - hi.astype(f32)
    mid = rest.astype(bf16)
    lo = (rest - mid.astype(f32)).astype(bf16)
    return hi, mid, lo


def iota(shape, dim):
    return lax.broadcasted_iota(i32, shape, dim)


def rows_to_xy(rows):
    i = rows - 12
    q = lax.shift_right_arithmetic(i * 2731, jnp.full(i.shape, 16, i32))
    return q - 4, i - q * 24 - 4


def own_rows(block, lo):
    return jnp.concatenate(
        [block[112 + 24 * x - lo : 112 + 24 * x - lo + 16] for x in range(16)], axis=0
    )


def wrap32(value):
    value &= 0xFFFFFFFF
    return value - (1 << 32) if value >= (1 << 31) else value


def rows(parts):
    return jnp.concatenate(parts, axis=0)


def lanes_of(parts):
    return jnp.concatenate(parts, axis=1)


MESH = pl.DeviceIdType.MESH
SEGMENTS = ((0, 0, 96, 304), (0, 1, 288, 496), (-1, 1, 64, 112), (1, 0, 480, 544))


def kernel(
    place,
    comm,
    seed_hbm,
    hop_hbm,
    mass_hbm,
    codes_hbm,
    table_hbm,
    sites_hbm,
    strength_hbm,
    left_hbm,
    *refs,
):
    if not comm:
        (halo_in, a1_in, a2_in, c_in), refs = refs[:4], refs[4:]
    (
        moments_ref,
        prev_ref,
        last_ref,
        seed_ref,
        hop_ref,
        mass_ref,
        codes_ref,
        table_ref,
        sites_ref,
        strength_ref,
        left_ref,
        halo_ref,
        wm_ref,
        wy_ref,
        w0_ref,
            hb_ref,
        mk_ref,
        sb_ref,
        f0_ref,
        f1_ref,
        f2_ref,
        a0_ref,
        a1_ref,
        a2_ref,
        b0_ref,
        b1_ref,
        b2_ref,
        c_ref,
        lt_ref,
        sel_ref,
        obc_ref,
        ob_ref,
        acc_ref,
        part_ref,
        got_ref,
        load_sem,
        send_sem,
        recv_sem,
        pair_send_sem,
        pair_recv_sem,
        send2_sem,
        recv2_sem,
    ) = refs
    gz, tx, ty = place()
    odd = gz % 2 == 1
    flip = gz % 2 * 2 - 1

    def z_of(p):
        return (3 * (1 - gz % 2)) + flip * (p - 1)

    if comm:
        near = [(dx, dy) for dx in (-1, 0, 1) for dy in (-1, 0, 1) if (dx, dy) != (0, 0)]
        outer = (gz + flip + 4) % 4
        inner = (gz - flip + 4) % 4
        tile = tx * 8 + ty
        column = tile // 4

        def neighbour(dx, dy, z):
            return {"gz": z, "xy": ((tx + dx + 8) % 8) * 8 + (ty + dy + 8) % 8}

        height = gz // 2 * 4 + tile % 4
        ring = sorted(range(1, 16), key=lambda k: -min(k // 2, 8 - k // 2))
        square = sorted(range(1, 16), key=lambda k: -min(k // 4, 4 - k // 4) - min(k % 4, 4 - k % 4))

        def along_z(step):
            k = ring[step - 1]
            high = (height + k // 2) % 8
            return {"gz": high // 4 * 2 + (gz + k) % 2, "xy": column * 4 + high % 4}

        def along_plane(step):
            k = square[step - 1]
            y, x = (column // 4 + k // 4) % 4, (column + k) % 4
            return {"gz": gz, "xy": (y * 4 + x) * 4 + tile % 4}

        barrier = pltpu.get_barrier_semaphore()
        partners = [neighbour(dx, dy, outer) for dx, dy in near]
        partners += [neighbour(dx, dy, gz) for dx, dy in near]
        partners += [f(step) for f in (along_z, along_plane) for step in range(1, 16)]
        for device in partners:
            pl.semaphore_signal(barrier, inc=1, device_id=device, device_id_type=MESH)

    loads = []
    for k, (src, dst) in enumerate(
        (
            (sites_hbm, sites_ref),
            (strength_hbm, strength_ref),
            (codes_hbm, codes_ref),
            (table_hbm, table_ref),
            (hop_hbm, hop_ref),
            (mass_hbm, mass_ref),
            (seed_hbm, seed_ref),
            (left_hbm, left_ref),
        )
    ):
        loads.append(pltpu.make_async_copy(src, dst, load_sem.at[k]))
        loads[-1].start()

    for load in loads[:4]:
        load.wait()
    codes = codes_ref[...]
    base = jnp.zeros((8, 128), f32)
    for level in range(4):
        base = jnp.where(codes == level, table_ref[level], base)
    site = sites_ref[...]
    lz = (site >> 14) - gz * 4
    lx = ((site >> 7) & 127) - tx * 16
    ly = (site & 127) - ty * 16
    inside = (lz >= 0) & (lz < 4) & (lx >= 0) & (lx < 16) & (ly >= 0) & (ly < 16)
    row = jnp.where(inside, lz * 2 + (lx >> 3), -1)
    col = (lx & 7) * 16 + ly
    pieces = split3(strength_ref[...])
    lhs, rhs = [], []
    for k in range(32):
        hit = jnp.broadcast_to(row[k : k + 1], (8, 128)) == iota((8, 128), 0)
        lhs.append(
            rows(
                [jnp.where(hit, jnp.broadcast_to(p[k : k + 1].astype(f32), (8, 128)), 0.0) for p in pieces]
                + [jnp.zeros((8, 128), f32)]
            ).astype(bf16)
        )
        at = jnp.broadcast_to(col[k : k + 1], (128, 128)) == iota((128, 128), 0)
        rhs.append(jnp.where(at, 1.0, 0.0).astype(bf16))
    added = lax.dot_general(lanes_of(lhs), lanes_of(rhs), NT, preferred_element_type=f32)
    onsite = base + (added[0:8] + added[8:16] + added[16:24])
    for h in range(2):
        up = [onsite[2 * z + h : 2 * z + h + 1] for z in range(4)]
        block = jnp.where(odd, rows(up), rows(up[::-1]))
        halo_ref[0, 4, h] = rows([block, jnp.zeros((4, 128), f32)])

    for load in loads[4:7]:
        load.wait()
    spread = jnp.where(iota((8, 128), 1) >> 4 == iota((8, 128), 0), 1.0, 0.0)
    mass_raw = mass_ref[...]
    mats = [0.5 * (mass_raw + mass_raw.T)]
    for d in range(3):
        mats += [hop_ref[d].T, hop_ref[d]]
    wide = jnp.dot(rows(mats) * 0.4, spread, precision=highest, preferred_element_type=f32)
    wide = [wide[8 * k : 8 * k + 8] for k in range(7)]
    same_r = (iota((16, 128), 1) & 15) == iota((16, 128), 0)

    def matrix(narrow):
        blocks = [jnp.where(same_r, jnp.broadcast_to(narrow[b : b + 1], (16, 128)), 0.0) for b in range(8)]
        return split2(rows(blocks))

    w_mass, w_xp, w_xm, w_yp, w_ym = [matrix(w) for w in wide[:5]]
    w_next = matrix(jnp.where(odd, wide[5], wide[6]))
    w_before = matrix(jnp.where(odd, wide[6], wide[5]))
    for slot, pair in enumerate((w_mass, w_xp, w_xm, w_next, w_before)):
        both = lanes_of(pair)
        wm_ref[256 * slot : 256 * slot + 128] = both
        wm_ref[256 * slot + 128 : 256 * slot + 256] = both
    for part in range(2):
        both = lanes_of([w_yp[part], w_ym[part]])
        wy_ref[256 * part : 256 * part + 128] = both
        wy_ref[256 * part + 128 : 256 * part + 256] = both
    w0_ref[0:128] = lanes_of(w_xp)
    w0_ref[128:256] = -lanes_of(w_xm)

    x, y = rows_to_xy(iota((576, 128), 0) + 8)
    lane = iota((576, 128), 1)
    xg = (tx * 16 + x + 128) & 127
    yg = ty * 16 + y
    lane1 = iota((1, 128), 1) & 15
    seeds = jnp.zeros((1, 128), i32)
    for r in range(16):
        seeds = jnp.where(lane1 == r, seed_ref[r], seeds)
    hb_ref[...] = ((xg * 128 + yg) * 8 + (lane >> 4)) * MULT + seeds
    mk_ref[...] = jnp.where((yg >= 0) & (yg < 128), 1.0, 0.0)

    def sign_plane(p, carry):
        zg = (gz * 4 + z_of(p) + 16) & 15
        word = hb_ref[...] + zg * wrap32(128 * 128 * 8 * MULT)
        word = word ^ lax.shift_right_logical(word, jnp.full(word.shape, 15, i32))
        word = word * -2048144789
        word = word ^ lax.shift_right_logical(word, jnp.full(word.shape, 13, i32))
        word = word * -1028477387
        mk = mk_ref[...]
        sb_ref[p] = jnp.where(word < 0, -mk, mk).astype(bf16)
        return carry

    lax.fori_loop(0, 9, sign_plane, 0)

    at = 0
    for dx, h, lo, hi in SEGMENTS:
        xr, yr = rows_to_xy(iota((hi - lo, 128), 0) + lo)
        xr = xr - 16 * dx - 8 * h
        ok = (xr >= 0) & (xr < 8)
        lane = iota((hi - lo, 128), 1)
        sels = []
        for dy in (-1, 0, 1):
            yy = yr - 16 * dy
            hit = ok & (yy >= 0) & (yy < 16) & (xr * 16 + yy == lane)
            sels.append(jnp.where(hit, 1.0, 0.0).astype(bf16))
        sel_ref[at : at + hi - lo] = lanes_of(sels)
        at += hi - lo

    fs = (f0_ref, f1_ref, f2_ref)
    as_ = (a0_ref, a1_ref, a2_ref)
    bs = (b0_ref, b1_ref, b2_ref)

    def keep(level, p, out, lo, hi):
        hi_f = out.astype(bf16).astype(f32)
        both = lanes_of([hi_f, out - hi_f])
        as_[level][p, lo:hi] = both.astype(bf16)
        bs[level][p, lo - 16 : hi] = rows([both[:8], both, both[:8]]).astype(bf16)

    def start(planes):
        lhs = []
        for p, radius in planes:
            lo, hi = LOHI[radius]
            lhs.append(lanes_of([sb_ref[p, lo + 16 : hi + 16], sb_ref[p, lo - 32 : hi - 32]]))
        prod = jnp.dot(rows(lhs), w0_ref[...], preferred_element_type=f32)
        prod = (prod[:, :128] + prod[:, 128:]) * 2.5
        at = 0
        for p, radius in planes:
            lo, hi = LOHI[radius]
            out = prod[at : at + hi - lo]
            at += hi - lo
            f0_ref[p, lo:hi] = out
            keep(0, p, out, lo, hi)

    start(((0, 2), (1, 3), (2, 3)))
    start(((3, 3), (4, 3), (5, 3)))
    start(((6, 2), (7, 1), (8, 0)))

    if comm:
        pl.semaphore_wait(barrier, len(partners))
        near_sends, far_sends = [], []
        for k, (dx, dy, far) in enumerate(
            [(dx, dy, True) for dx, dy in near] + [(0, 0, True)] + [(dx, dy, False) for dx, dy in near]
        ):
            send = pltpu.make_async_remote_copy(
                src_ref=halo_ref.at[0, 4],
                dst_ref=halo_ref.at[int(far), (1 - dx) * 3 + 1 - dy],
                send_sem=send_sem.at[k],
                recv_sem=recv_sem.at[k],
                device_id=neighbour(dx, dy, outer if far else gz),
                device_id_type=MESH,
            )
            send.start()
            (far_sends if far else near_sends).append(send)

    loads[7].wait()

    def turn_left(p, carry):
        for m in range(3):
            for h in range(2):
                lt_ref[m, p - 1, 128 * h : 128 * h + 128] = left_ref[m, pl.ds(2 * z_of(p) + h, 128, stride=8), :].T
        return carry

    lax.fori_loop(1, 5, turn_left, 0)
    acc_ref[...] = jnp.zeros(acc_ref.shape, f32)

    def halves(both):
        return both[:, :128] + both[:, 128:]

    def add_moments(n, p, velocity):
        for m in range(3):
            prod = lt_ref[m, p - 1] * velocity
            tot = prod[0:8]
            for k in range(8, 256, 8):
                tot = tot + prod[k : k + 8]
            acc_ref[m * 4 + n] += tot

    def hop(n, planes):
        a_ref, b_ref = as_[n], bs[n]
        lhs, nxt, before, ylhs = [], [], [], []
        for p, radius in planes:
            lo, hi = LOHI[radius]
            lhs.append(lanes_of([a_ref[p, lo:hi], b_ref[p, lo + 16 : hi + 16], b_ref[p, lo - 32 : hi - 32]]))
            nxt.append(a_ref[p + 1, lo:hi])
            before.append(a_ref[p - 1, lo:hi])
            first = 0 if radius == 1 else 16
            ylhs.append(a_ref[p, lo - first : hi + 16 - first])
        own = planes[0][0] <= 4
        if own:
            main = halves(jnp.dot(rows(lhs), wm_ref[0:768], preferred_element_type=f32))
            nxt = halves(jnp.dot(rows(nxt), wm_ref[768:1024], preferred_element_type=f32))
            before = halves(jnp.dot(rows(before), wm_ref[1024:1280], preferred_element_type=f32))
        else:
            all_lhs = lanes_of([rows(lhs), rows(nxt), rows(before)])
            main = halves(jnp.dot(all_lhs, wm_ref[...], preferred_element_type=f32))
        ylhs = rows(ylhs)
        yy = jnp.dot(lanes_of([ylhs, ylhs]), wy_ref[...], preferred_element_type=f32)
        yp = pltpu.roll(yy[:, :128], yy.shape[0] - 1, 0)
        ym = pltpu.roll(yy[:, 128:], 1, 0)
        outs, r, s = [], 0, 0
        for p, radius in planes:
            lo, hi = LOHI[radius]
            first = 0 if radius == 1 else 16
            size, t = hi - lo, s + first
            out = main[r : r + size] + yp[t : t + size] + ym[t : t + size]
            if own:
                up, down = nxt[r : r + size], before[r : r + size]
                out = out + up + down
                if p <= 4:
                    add_moments(n, p, own_rows(up, lo) - own_rows(down, lo))
            outs.append(out)
            r += size
            s += size + 16
        return outs

    def first_hop(planes):
        for (p, radius), out in zip(planes, hop(0, planes)):
            lo, hi = LOHI[radius]
            f1_ref[p, lo:hi] = out

    first_hop(((1, 2), (2, 2), (3, 2), (4, 2)))
    first_hop(((5, 2), (6, 1), (7, 0)))

    def energies(far, planes):
        obc_ref[...] = jnp.zeros(obc_ref.shape, f32)
        at = 0
        for dx, h, lo, hi in SEGMENTS:
            sels, vals = [], []
            for dy in (-1, 0, 1):
                sel = sel_ref[at : at + hi - lo, 128 * (dy + 1) : 128 * (dy + 2)]
                block = halo_ref[far, (dx + 1) * 3 + dy + 1, h]
                for piece in split3(rows([block, jnp.zeros((8, 128), f32)])):
                    sels.append(sel)
                    vals.append(piece)
            at += hi - lo
            obc_ref[lo - 64 : hi - 64] += lax.dot_general(
                lanes_of(sels), lanes_of(vals), NT, preferred_element_type=f32
            )
        for p, col in planes:
            ob_ref[p] = jnp.broadcast_to(obc_ref[:, col : col + 1] * 0.4, (480, 128))

    def site_term(n, p, lo, hi):
        return ob_ref[p, lo - 64 : hi - 64] * fs[n][p, lo:hi]

    def first_rest(planes):
        for p, radius in planes:
            lo, hi = LOHI[radius]
            out = (f1_ref[p, lo:hi] + site_term(0, p, lo, hi)) * (mk_ref[lo - 8 : hi - 8] * 0.5)
            f1_ref[p, lo:hi] = out
            keep(1, p, out, lo, hi)

    def step(n, planes):
        for (p, radius), out in zip(planes, hop(n, planes)):
            lo, hi = LOHI[radius]
            out = (out + site_term(n, p, lo, hi)) * mk_ref[lo - 8 : hi - 8] - fs[n - 1][p, lo:hi]
            if n == 1:
                f2_ref[p, lo:hi] = out
                keep(2, p, out, lo, hi)
            else:
                v = own_rows(out, lo)
                hi_f = v.astype(bf16).astype(f32)
                c_ref[p] = lanes_of([hi_f, v - hi_f]).astype(bf16)
                f0_ref[p, 0:256] = v

    pair_sends = []

    def to_pair(level):
        if not comm:
            if level < 3:
                as_[level][0] = (a1_in, a2_in)[level - 1][...]
            else:
                c_ref[0] = c_in[2]
            return
        if level < 3:
            lo, hi = LOHI[2 - level]
            face = as_[level].at[:, pl.ds(lo, hi - lo)]
        else:
            face = c_ref
        pair_sends.append(
            pltpu.make_async_remote_copy(
                src_ref=face.at[1],
                dst_ref=face.at[0],
                send_sem=pair_send_sem.at[level - 1],
                recv_sem=pair_recv_sem.at[level - 1],
                device_id={"gz": inner, "xy": tile},
                device_id_type=MESH,
            )
        )
        pair_sends[-1].start()

    def from_pair():
        for send in pair_sends:
            send.wait()
        del pair_sends[:]

    if comm:
        for send in near_sends:
            send.wait()
    else:
        halo_ref[...] = halo_in[...]
    energies(0, [(p, p - 1) for p in range(1, 5)])
    first_rest(((1, 2),))
    to_pair(1)
    first_rest(((2, 2), (3, 2), (4, 2)))
    step(1, ((2, 1), (3, 1)))
    from_pair()
    step(1, ((1, 1),))
    to_pair(2)
    if comm:
        for send in far_sends:
            send.wait()
    energies(1, [(p, 8 - p) for p in range(5, 8)])
    first_rest(((5, 2), (6, 1), (7, 0)))
    step(1, ((4, 1), (5, 1), (6, 0)))
    from_pair()
    step(2, ((1, 0), (2, 0)))
    to_pair(3)
    step(2, ((3, 0), (4, 0), (5, 0)))

    def z_product(slot, planes):
        lhs = rows([c_ref[p] for p in planes])
        return halves(jnp.dot(lhs, wm_ref[256 * slot : 256 * slot + 256], preferred_element_type=f32))

    nxt = z_product(3, (2, 3, 4, 5))
    before = z_product(4, (1, 2, 3))
    for p in (2, 3, 4):
        add_moments(3, p, nxt[256 * p - 256 : 256 * p] - before[256 * p - 512 : 256 * p - 256])
    from_pair()
    add_moments(3, 1, nxt[:256] - z_product(4, (0,)))

    fold = jnp.where((iota((128, 128), 0) & 15) == (iota((128, 128), 1) & 15), 1.0, 0.0)
    folded = jnp.dot(acc_ref[...].reshape(96, 128), fold, precision=highest, preferred_element_type=f32)
    mine = (iota((96, 128), 1) >> 4) == ((iota((96, 128), 0) >> 3) & 7)
    folded = jnp.where(mine, folded, 0.0) * (flip.astype(f32) * (2.5 / math.sqrt(8 * 262144)))
    part = rows([jnp.sum(folded[:64], axis=0, keepdims=True), jnp.sum(folded[64:], axis=0, keepdims=True)])
    part_ref[0] = part

    def send_part(stage, target):
        copies = []
        for step in range(1, 16):
            copy = pltpu.make_async_remote_copy(
                src_ref=part_ref.at[stage],
                dst_ref=got_ref.at[stage, step - 1],
                send_sem=send2_sem.at[stage, step - 1],
                recv_sem=recv2_sem.at[stage, step - 1],
                device_id=target(step),
                device_id_type=MESH,
            )
            copy.start()
            copies.append(copy)
        return copies

    def add_parts(stage, copies, total):
        for copy in copies:
            copy.wait()
        for step in range(1, 16):
            total = total + got_ref[stage, step - 1]
        return total

    if comm:
        copies = send_part(0, along_z)

    def plane_out(p, carry):
        last = f0_ref[p, 0:256].T
        prev = own_rows(f2_ref[p, 80:512], 80).T
        for h in range(2):
            place_of = pl.ds(2 * z_of(p) + h, 128, stride=8)
            last_ref[place_of, :] = last[:, 128 * h : 128 * h + 128]
            prev_ref[place_of, :] = prev[:, 128 * h : 128 * h + 128]
        return carry

    lax.fori_loop(1, 5, plane_out, 0)

    if comm:
        part = add_parts(0, copies, part)
        part_ref[1] = part
        part = add_parts(1, send_part(1, along_plane), part)
    for k in range(12):
        moments_ref[k // 4, k % 4 : k % 4 + 1, :] = part[k // 8 : k // 8 + 1, 16 * (k % 8) : 16 * (k % 8) + 16]


def whole(place, comm, *operands):
    hbm = pl.BlockSpec(memory_space=pltpu.HBM)
    vm = pl.BlockSpec(memory_space=pltpu.VMEM)
    plane = lambda kind, lanes: pltpu.VMEM((9, NR, lanes), kind)
    dma = pltpu.SemaphoreType.DMA
    extra = {"collective_id": 0, "has_side_effects": True} if comm else {}
    return pl.pallas_call(
        functools.partial(kernel, place, comm),
        out_shape=(
            jax.ShapeDtypeStruct((3, 4, 16), f32),
            jax.ShapeDtypeStruct((1024, 128), f32),
            jax.ShapeDtypeStruct((1024, 128), f32),
        ),
        in_specs=[hbm] * 8 + [vm] * (len(operands) - 8),
        out_specs=(vm, vm, vm),
        scratch_shapes=[
            pltpu.SMEM((16,), i32),
            pltpu.VMEM((3, 8, 8), f32),
            pltpu.VMEM((8, 8), f32),
            pltpu.VMEM((8, 128), i32),
            pltpu.SMEM((4,), f32),
            pltpu.VMEM((32, 128), i32),
            pltpu.VMEM((32, 128), f32),
            pltpu.VMEM((3, 1024, 128), f32),
            pltpu.VMEM((2, 9, 2, 8, 128), f32),
            pltpu.VMEM((1280, 256), bf16),
            pltpu.VMEM((512, 256), bf16),
            pltpu.VMEM((256, 256), bf16),
            pltpu.VMEM((576, 128), i32),
            pltpu.VMEM((576, 128), f32),
            pltpu.VMEM((9, 576, 128), bf16),
            plane(f32, 128),
            plane(f32, 128),
            plane(f32, 128),
            plane(bf16, 256),
            plane(bf16, 256),
            plane(bf16, 256),
            plane(bf16, 256),
            plane(bf16, 256),
            plane(bf16, 256),
            pltpu.VMEM((6, 256, 256), bf16),
            pltpu.VMEM((3, 4, 256, 128), f32),
            pltpu.VMEM((528, 384), bf16),
            pltpu.VMEM((480, 16), f32),
            pltpu.VMEM((8, 480, 128), f32),
            pltpu.VMEM((12, 8, 128), f32),
            pltpu.VMEM((2, 2, 128), f32),
            pltpu.VMEM((2, 15, 2, 128), f32),
            dma((8,)),
            dma((17,)),
            dma((17,)),
            dma((3,)),
            dma((3,)),
            dma((2, 15)),
            dma((2, 15)),
        ],
        compiler_params=pltpu.CompilerParams(vmem_limit_bytes=48 * 1024 * 1024, **extra),
        name="chain",
    )(*[pltpu.with_memory_space_constraint(a, pltpu.HBM) for a in operands[:8]], *operands[8:])


def copy_kernel(a_ref, b_ref, c_ref, a_out, b_out, c_out):
    a_out[...] = a_ref[...]
    b_out[...] = b_ref[...]
    c_out[...] = c_ref[...]


def copied(*arrays):
    spec = pl.BlockSpec(memory_space=pltpu.VMEM)
    return pl.pallas_call(
        copy_kernel,
        out_shape=[jax.ShapeDtypeStruct(a.shape, a.dtype) for a in arrays],
        in_specs=[spec] * 3,
        out_specs=[spec] * 3,
        compiler_params=pltpu.CompilerParams(vmem_limit_bytes=48 * 1024 * 1024),
        name="copied",
    )(*arrays)


def where_am_i():
    tile = lax.axis_index("xy")
    return lax.axis_index("gz"), tile // 8, tile % 8


def per_device(
    left_vectors,
    sign_seeds,
    level_codes,
    level_table,
    disorder_sites,
    disorder_strength,
    hoppings,
    mass_raw,
):
    moments, prev, last = whole(
        where_am_i,
        True,
        sign_seeds,
        hoppings,
        mass_raw,
        level_codes.reshape(8, 128),
        level_table,
        disorder_sites.reshape(32, 128),
        disorder_strength.reshape(32, 128),
        left_vectors.reshape(3, 1024, 128),
    )
    moments, prev, last = copied(moments, prev, last)
    shape = left_vectors.shape[1:]
    return moments, prev.reshape(shape), last.reshape(shape)


def solution(mesh):
    in_specs = (
        P(None, None, None, "gz", "xy", None),
        P(),
        P("gz", "xy", None),
        P(),
        P(),
        P(),
        P(),
        P(),
    )
    out_specs = (P(), P(None, None, "gz", "xy", None), P(None, None, "gz", "xy", None))
    return jax.shard_map(
        per_device, mesh=mesh, in_specs=in_specs, out_specs=out_specs, check_vma=False
    )
```

```python
import functools
import math

import jax
import jax.numpy as jnp
from jax import lax
from jax.experimental import pallas as pl
from jax.experimental.pallas import tpu as pltpu
from jax.sharding import PartitionSpec as P

f32, bf16, i32 = jnp.float32, jnp.bfloat16, jnp.int32

PITCH = 24
NR = 608
LOHI = {0: (112, 496), 1: (80, 512), 2: (64, 544), 3: (32, 560)}
MULT = 668265261
NT = (((1,), (1,)), ((), ()))
highest = lax.Precision.HIGHEST


def split2(v):
    hi = v.astype(bf16)
    lo = (v - hi.astype(f32)).astype(bf16)
    return hi, lo


def split3(v):
    hi = v.astype(bf16)
    rest = v - hi.astype(f32)
    mid = rest.astype(bf16)
    lo = (rest - mid.astype(f32)).astype(bf16)
    return hi, mid, lo


def iota(shape, dim):
    return lax.broadcasted_iota(i32, shape, dim)


def rows_to_xy(rows):
    i = rows - 12
    q = lax.shift_right_arithmetic(i * 2731, jnp.full(i.shape, 16, i32))
    return q - 4, i - q * 24 - 4


def own_rows(block, lo):
    return jnp.concatenate(
        [block[112 + 24 * x - lo : 112 + 24 * x - lo + 16] for x in range(16)], axis=0
    )


def wrap32(value):
    value &= 0xFFFFFFFF
    return value - (1 << 32) if value >= (1 << 31) else value


def rows(parts):
    return jnp.concatenate(parts, axis=0)


def lanes_of(parts):
    return jnp.concatenate(parts, axis=1)


MESH = pl.DeviceIdType.MESH
SEGMENTS = ((0, 0, 96, 304), (0, 1, 288, 496), (-1, 1, 64, 112), (1, 0, 480, 544))


def kernel(
    place,
    comm,
    seed_hbm,
    hop_hbm,
    mass_hbm,
    codes_hbm,
    table_hbm,
    sites_hbm,
    strength_hbm,
    left_hbm,
    *refs,
):
    if not comm:
        (halo_in, a1_in, a2_in, c_in), refs = refs[:4], refs[4:]
    (
        moments_ref,
        prev_ref,
        last_ref,
        seed_ref,
        hop_ref,
        mass_ref,
        codes_ref,
        table_ref,
        sites_ref,
        strength_ref,
        left_ref,
        halo_ref,
        wm_ref,
        wy_ref,
        w0_ref,
            hb_ref,
        mk_ref,
        sb_ref,
        f0_ref,
        f1_ref,
        f2_ref,
        a0_ref,
        a1_ref,
        a2_ref,
        b0_ref,
        b1_ref,
        b2_ref,
        c_ref,
        lt_ref,
        sel_ref,
        obc_ref,
        ob_ref,
        acc_ref,
        part_ref,
        got_ref,
        load_sem,
        send_sem,
        recv_sem,
        pair_send_sem,
        pair_recv_sem,
        send2_sem,
        recv2_sem,
    ) = refs
    gz, tx, ty = place()
    odd = gz % 2 == 1
    flip = gz % 2 * 2 - 1

    def z_of(p):
        return (3 * (1 - gz % 2)) + flip * (p - 1)

    def await_copies(whole_ref, sem):
        pltpu.make_async_copy(whole_ref, whole_ref, sem).wait()

    if comm:
        near = [(dx, dy) for dx in (-1, 0, 1) for dy in (-1, 0, 1) if (dx, dy) != (0, 0)]
        outer = (gz + flip + 4) % 4
        inner = (gz - flip + 4) % 4
        tile = tx * 8 + ty
        column = tile // 4

        def neighbour(dx, dy, z):
            return {"gz": z, "xy": ((tx + dx + 8) % 8) * 8 + (ty + dy + 8) % 8}

        height = gz // 2 * 4 + tile % 4
        ring = sorted(range(1, 16), key=lambda k: -min(k // 2, 8 - k // 2))
        square = sorted(range(1, 16), key=lambda k: -min(k // 4, 4 - k // 4) - min(k % 4, 4 - k % 4))

        def along_z(step):
            k = ring[step - 1]
            high = (height + k // 2) % 8
            return {"gz": high // 4 * 2 + (gz + k) % 2, "xy": column * 4 + high % 4}

        def along_plane(step):
            k = square[step - 1]
            y, x = (column // 4 + k // 4) % 4, (column + k) % 4
            return {"gz": gz, "xy": (y * 4 + x) * 4 + tile % 4}

        barrier = pltpu.get_barrier_semaphore()
        partners = [neighbour(dx, dy, outer) for dx, dy in near]
        partners += [neighbour(dx, dy, gz) for dx, dy in near]
        partners += [f(step) for f in (along_z, along_plane) for step in range(1, 16)]
        for device in partners:
            pl.semaphore_signal(barrier, inc=1, device_id=device, device_id_type=MESH)

    loads = []
    for k, (src, dst) in enumerate(
        (
            (sites_hbm, sites_ref),
            (strength_hbm, strength_ref),
            (codes_hbm, codes_ref),
            (table_hbm, table_ref),
            (hop_hbm, hop_ref),
            (mass_hbm, mass_ref),
            (seed_hbm, seed_ref),
            (left_hbm, left_ref),
        )
    ):
        loads.append(pltpu.make_async_copy(src, dst, load_sem.at[k]))
        loads[-1].start()

    for load in loads[:4]:
        load.wait()
    codes = codes_ref[...]
    base = jnp.zeros((8, 128), f32)
    for level in range(4):
        base = jnp.where(codes == level, table_ref[level], base)
    site = sites_ref[...]
    lz = (site >> 14) - gz * 4
    lx = ((site >> 7) & 127) - tx * 16
    ly = (site & 127) - ty * 16
    inside = (lz >= 0) & (lz < 4) & (lx >= 0) & (lx < 16) & (ly >= 0) & (ly < 16)
    row = jnp.where(inside, lz * 2 + (lx >> 3), -1)
    col = (lx & 7) * 16 + ly
    pieces = split3(strength_ref[...])
    lhs, rhs = [], []
    for k in range(32):
        hit = jnp.broadcast_to(row[k : k + 1], (8, 128)) == iota((8, 128), 0)
        lhs.append(
            rows(
                [jnp.where(hit, jnp.broadcast_to(p[k : k + 1].astype(f32), (8, 128)), 0.0) for p in pieces]
                + [jnp.zeros((8, 128), f32)]
            ).astype(bf16)
        )
        at = jnp.broadcast_to(col[k : k + 1], (128, 128)) == iota((128, 128), 0)
        rhs.append(jnp.where(at, 1.0, 0.0).astype(bf16))
    added = lax.dot_general(lanes_of(lhs), lanes_of(rhs), NT, preferred_element_type=f32)
    onsite = base + (added[0:8] + added[8:16] + added[16:24])
    for h in range(2):
        up = [onsite[2 * z + h : 2 * z + h + 1] for z in range(4)]
        block = jnp.where(odd, rows(up), rows(up[::-1]))
        halo_ref[0, 8 + h] = block

    for load in loads[4:7]:
        load.wait()
    spread = jnp.where(iota((8, 128), 1) >> 4 == iota((8, 128), 0), 1.0, 0.0)
    mass_raw = mass_ref[...]
    mats = [0.5 * (mass_raw + mass_raw.T)]
    for d in range(3):
        mats += [hop_ref[d].T, hop_ref[d]]
    wide = jnp.dot(rows(mats) * 0.4, spread, precision=highest, preferred_element_type=f32)
    wide = [wide[8 * k : 8 * k + 8] for k in range(7)]
    same_r = (iota((16, 128), 1) & 15) == iota((16, 128), 0)

    def matrix(narrow):
        blocks = [jnp.where(same_r, jnp.broadcast_to(narrow[b : b + 1], (16, 128)), 0.0) for b in range(8)]
        return split2(rows(blocks))

    w_mass, w_xp, w_xm, w_yp, w_ym = [matrix(w) for w in wide[:5]]
    w_next = matrix(jnp.where(odd, wide[5], wide[6]))
    w_before = matrix(jnp.where(odd, wide[6], wide[5]))
    for slot, pair in enumerate((w_mass, w_xp, w_xm, w_next, w_before)):
        both = lanes_of(pair)
        wm_ref[256 * slot : 256 * slot + 128] = both
        wm_ref[256 * slot + 128 : 256 * slot + 256] = both
    for part in range(2):
        both = lanes_of([w_yp[part], w_ym[part]])
        wy_ref[256 * part : 256 * part + 128] = both
        wy_ref[256 * part + 128 : 256 * part + 256] = both
    w0_ref[0:128] = lanes_of(w_xp)
    w0_ref[128:256] = -lanes_of(w_xm)

    x, y = rows_to_xy(iota((576, 128), 0) + 8)
    lane = iota((576, 128), 1)
    xg = (tx * 16 + x + 128) & 127
    yg = ty * 16 + y
    lane1 = iota((1, 128), 1) & 15
    seeds = jnp.zeros((1, 128), i32)
    for r in range(16):
        seeds = jnp.where(lane1 == r, seed_ref[r], seeds)
    hb_ref[...] = ((xg * 128 + yg) * 8 + (lane >> 4)) * MULT + seeds
    mk_ref[...] = jnp.where((yg >= 0) & (yg < 128), 1.0, 0.0)

    def sign_plane(p, carry):
        zg = (gz * 4 + z_of(p) + 16) & 15
        word = hb_ref[...] + zg * wrap32(128 * 128 * 8 * MULT)
        word = word ^ lax.shift_right_logical(word, jnp.full(word.shape, 15, i32))
        word = word * -2048144789
        word = word ^ lax.shift_right_logical(word, jnp.full(word.shape, 13, i32))
        word = word * -1028477387
        mk = mk_ref[...]
        sb_ref[p] = jnp.where(word < 0, -mk, mk).astype(bf16)
        return carry

    lax.fori_loop(0, 9, sign_plane, 0)

    at = 0
    for dx, h, lo, hi in SEGMENTS:
        xr, yr = rows_to_xy(iota((hi - lo, 128), 0) + lo)
        xr = xr - 16 * dx - 8 * h
        ok = (xr >= 0) & (xr < 8)
        lane = iota((hi - lo, 128), 1)
        sels = []
        for dy in (-1, 0, 1):
            yy = yr - 16 * dy
            hit = ok & (yy >= 0) & (yy < 16) & (xr * 16 + yy == lane)
            sels.append(jnp.where(hit, 1.0, 0.0).astype(bf16))
        sel_ref[at : at + hi - lo] = lanes_of(sels)
        at += hi - lo

    fs = (f0_ref, f1_ref, f2_ref)
    as_ = (a0_ref, a1_ref, a2_ref)
    bs = (b0_ref, b1_ref, b2_ref)

    def keep(level, p, out, lo, hi):
        hi_f = out.astype(bf16).astype(f32)
        both = lanes_of([hi_f, out - hi_f])
        as_[level][p, lo:hi] = both.astype(bf16)
        bs[level][p, lo - 16 : hi] = rows([both[:8], both, both[:8]]).astype(bf16)

    def start(planes):
        lhs = []
        for p, radius in planes:
            lo, hi = LOHI[radius]
            lhs.append(lanes_of([sb_ref[p, lo + 16 : hi + 16], sb_ref[p, lo - 32 : hi - 32]]))
        prod = jnp.dot(rows(lhs), w0_ref[...], preferred_element_type=f32)
        prod = (prod[:, :128] + prod[:, 128:]) * 2.5
        at = 0
        for p, radius in planes:
            lo, hi = LOHI[radius]
            out = prod[at : at + hi - lo]
            at += hi - lo
            f0_ref[p, lo:hi] = out
            keep(0, p, out, lo, hi)

    start(((0, 2), (1, 3), (2, 3)))
    if comm:
        pl.semaphore_wait(barrier, len(partners))
        for dx, dy, far in (
            [(dx, dy, True) for dx, dy in near] + [(0, 0, True)] + [(dx, dy, False) for dx, dy in near]
        ):
            first, count = (1 if dx > 0 else 0, 1) if dx else (0, 2)
            there = 2 * ((1 - dx) * 3 + 1 - dy) + first
            pltpu.make_async_remote_copy(
                src_ref=halo_ref.at[0, pl.ds(8 + first, count)],
                dst_ref=halo_ref.at[int(far), pl.ds(there, count)],
                send_sem=send_sem,
                recv_sem=recv_sem.at[int(far)],
                device_id=neighbour(dx, dy, outer if far else gz),
                device_id_type=MESH,
            ).start()

    start(((3, 3), (4, 3), (5, 3)))
    start(((6, 2), (7, 1), (8, 0)))

    loads[7].wait()

    def turn_left(p, carry):
        for m in range(3):
            for h in range(2):
                lt_ref[m, p - 1, 128 * h : 128 * h + 128] = left_ref[m, pl.ds(2 * z_of(p) + h, 128, stride=8), :].T
        return carry

    lax.fori_loop(1, 5, turn_left, 0)
    acc_ref[...] = jnp.zeros(acc_ref.shape, f32)

    def halves(both):
        return both[:, :128] + both[:, 128:]

    def add_moments(n, p, velocity):
        for m in range(3):
            prod = lt_ref[m, p - 1] * velocity
            tot = prod[0:8]
            for k in range(8, 256, 8):
                tot = tot + prod[k : k + 8]
            acc_ref[m * 4 + n] += tot

    def hop(n, planes):
        a_ref, b_ref = as_[n], bs[n]
        lhs, nxt, before, ylhs = [], [], [], []
        for p, radius in planes:
            lo, hi = LOHI[radius]
            lhs.append(lanes_of([a_ref[p, lo:hi], b_ref[p, lo + 16 : hi + 16], b_ref[p, lo - 32 : hi - 32]]))
            nxt.append(a_ref[p + 1, lo:hi])
            before.append(a_ref[p - 1, lo:hi])
            first = 0 if radius == 1 else 16
            ylhs.append(a_ref[p, lo - first : hi + 16 - first])
        own = planes[0][0] <= 4
        if own:
            main = halves(jnp.dot(rows(lhs), wm_ref[0:768], preferred_element_type=f32))
            nxt = halves(jnp.dot(rows(nxt), wm_ref[768:1024], preferred_element_type=f32))
            before = halves(jnp.dot(rows(before), wm_ref[1024:1280], preferred_element_type=f32))
        else:
            all_lhs = lanes_of([rows(lhs), rows(nxt), rows(before)])
            main = halves(jnp.dot(all_lhs, wm_ref[...], preferred_element_type=f32))
        ylhs = rows(ylhs)
        yy = jnp.dot(lanes_of([ylhs, ylhs]), wy_ref[...], preferred_element_type=f32)
        yp = pltpu.roll(yy[:, :128], yy.shape[0] - 1, 0)
        ym = pltpu.roll(yy[:, 128:], 1, 0)
        outs, r, s = [], 0, 0
        for p, radius in planes:
            lo, hi = LOHI[radius]
            first = 0 if radius == 1 else 16
            size, t = hi - lo, s + first
            out = main[r : r + size] + yp[t : t + size] + ym[t : t + size]
            if own:
                up, down = nxt[r : r + size], before[r : r + size]
                out = out + up + down
                if p <= 4:
                    add_moments(n, p, own_rows(up, lo) - own_rows(down, lo))
            outs.append(out)
            r += size
            s += size + 16
        return outs

    def first_hop(planes):
        for (p, radius), out in zip(planes, hop(0, planes)):
            lo, hi = LOHI[radius]
            f1_ref[p, lo:hi] = out

    first_hop(((1, 2), (2, 2), (3, 2), (4, 2)))
    first_hop(((5, 2), (6, 1), (7, 0)))

    def energies(far, planes):
        obc_ref[...] = jnp.zeros(obc_ref.shape, f32)
        at = 0
        for dx, h, lo, hi in SEGMENTS:
            sels, vals = [], []
            for dy in (-1, 0, 1):
                sel = sel_ref[at : at + hi - lo, 128 * (dy + 1) : 128 * (dy + 2)]
                block = halo_ref[far, 2 * ((dx + 1) * 3 + dy + 1) + h]
                for piece in split3(rows([block, jnp.zeros((12, 128), f32)])):
                    sels.append(sel)
                    vals.append(piece)
            at += hi - lo
            obc_ref[lo - 64 : hi - 64] += lax.dot_general(
                lanes_of(sels), lanes_of(vals), NT, preferred_element_type=f32
            )
        for p, col in planes:
            ob_ref[p] = jnp.broadcast_to(obc_ref[:, col : col + 1] * 0.4, (480, 128))

    def site_term(n, p, lo, hi):
        return ob_ref[p, lo - 64 : hi - 64] * fs[n][p, lo:hi]

    def first_rest(planes):
        for p, radius in planes:
            lo, hi = LOHI[radius]
            out = (f1_ref[p, lo:hi] + site_term(0, p, lo, hi)) * (mk_ref[lo - 8 : hi - 8] * 0.5)
            f1_ref[p, lo:hi] = out
            keep(1, p, out, lo, hi)

    def step(n, planes):
        for (p, radius), out in zip(planes, hop(n, planes)):
            lo, hi = LOHI[radius]
            out = (out + site_term(n, p, lo, hi)) * mk_ref[lo - 8 : hi - 8] - fs[n - 1][p, lo:hi]
            if n == 1:
                f2_ref[p, lo:hi] = out
                keep(2, p, out, lo, hi)
            else:
                v = own_rows(out, lo)
                hi_f = v.astype(bf16).astype(f32)
                c_ref[p] = lanes_of([hi_f, v - hi_f]).astype(bf16)
                f0_ref[p, 0:256] = v

    pair_sends = []

    def to_pair(level):
        if not comm:
            if level < 3:
                as_[level][0] = (a1_in, a2_in)[level - 1][...]
            else:
                c_ref[0] = c_in[2]
            return
        if level < 3:
            lo, hi = LOHI[2 - level]
            face = as_[level].at[:, pl.ds(lo, hi - lo)]
        else:
            face = c_ref
        pair_sends.append(
            pltpu.make_async_remote_copy(
                src_ref=face.at[1],
                dst_ref=face.at[0],
                send_sem=pair_send_sem.at[level - 1],
                recv_sem=pair_recv_sem.at[level - 1],
                device_id={"gz": inner, "xy": tile},
                device_id_type=MESH,
            )
        )
        pair_sends[-1].start()

    def from_pair():
        for send in pair_sends:
            send.wait()
        del pair_sends[:]

    if comm:
        await_copies(halo_ref.at[0, pl.ds(0, 10)], recv_sem.at[0])
    else:
        halo_ref[...] = halo_in[...]
    energies(0, [(p, p - 1) for p in range(1, 5)])
    first_rest(((1, 2),))
    to_pair(1)
    first_rest(((2, 2), (3, 2), (4, 2)))
    step(1, ((2, 1), (3, 1)))
    from_pair()
    step(1, ((1, 1),))
    to_pair(2)
    if comm:
        await_copies(halo_ref.at[1, pl.ds(0, 12)], recv_sem.at[1])
    energies(1, [(p, 8 - p) for p in range(5, 8)])
    first_rest(((5, 2), (6, 1), (7, 0)))
    step(1, ((4, 1), (5, 1), (6, 0)))
    from_pair()
    step(2, ((1, 0), (2, 0)))
    to_pair(3)
    step(2, ((3, 0), (4, 0), (5, 0)))

    def z_product(slot, planes):
        lhs = rows([c_ref[p] for p in planes])
        return halves(jnp.dot(lhs, wm_ref[256 * slot : 256 * slot + 256], preferred_element_type=f32))

    nxt = z_product(3, (2, 3, 4, 5))
    before = z_product(4, (1, 2, 3))
    for p in (2, 3, 4):
        add_moments(3, p, nxt[256 * p - 256 : 256 * p] - before[256 * p - 512 : 256 * p - 256])
    from_pair()
    add_moments(3, 1, nxt[:256] - z_product(4, (0,)))

    fold = jnp.where((iota((128, 128), 0) & 15) == (iota((128, 128), 1) & 15), 1.0, 0.0)
    folded = jnp.dot(acc_ref[...].reshape(96, 128), fold, precision=highest, preferred_element_type=f32)
    mine = (iota((96, 128), 1) >> 4) == ((iota((96, 128), 0) >> 3) & 7)
    folded = jnp.where(mine, folded, 0.0) * (flip.astype(f32) * (2.5 / math.sqrt(8 * 262144)))
    part = rows([jnp.sum(folded[:64], axis=0, keepdims=True), jnp.sum(folded[64:], axis=0, keepdims=True)])
    part_ref[0] = part

    def send_part(stage, target):
        for step in range(1, 16):
            pltpu.make_async_remote_copy(
                src_ref=part_ref.at[stage],
                dst_ref=got_ref.at[stage, step - 1],
                send_sem=send2_sem.at[stage],
                recv_sem=recv2_sem.at[stage],
                device_id=target(step),
                device_id_type=MESH,
            ).start()

    def add_parts(stage, total):
        await_copies(got_ref.at[stage], recv2_sem.at[stage])
        return total + jnp.sum(got_ref[stage], axis=0)

    if comm:
        send_part(0, along_z)

    def plane_out(p, carry):
        last = f0_ref[p, 0:256].T
        prev = own_rows(f2_ref[p, 80:512], 80).T
        for h in range(2):
            place_of = pl.ds(2 * z_of(p) + h, 128, stride=8)
            last_ref[place_of, :] = last[:, 128 * h : 128 * h + 128]
            prev_ref[place_of, :] = prev[:, 128 * h : 128 * h + 128]
        return carry

    lax.fori_loop(1, 5, plane_out, 0)

    if comm:
        part = add_parts(0, part)
        part_ref[1] = part
        send_part(1, along_plane)
        part = add_parts(1, part)
        await_copies(halo_ref.at[0, pl.ds(0, 10)], send_sem)
        await_copies(halo_ref.at[1, pl.ds(0, 12)], send_sem)
        await_copies(got_ref.at[0], send2_sem.at[0])
        await_copies(got_ref.at[1], send2_sem.at[1])
    for k in range(12):
        moments_ref[k // 4, k % 4 : k % 4 + 1, :] = part[k // 8 : k // 8 + 1, 16 * (k % 8) : 16 * (k % 8) + 16]


def whole(place, comm, *operands):
    hbm = pl.BlockSpec(memory_space=pltpu.HBM)
    vm = pl.BlockSpec(memory_space=pltpu.VMEM)
    plane = lambda kind, lanes: pltpu.VMEM((9, NR, lanes), kind)
    dma = pltpu.SemaphoreType.DMA
    extra = {"collective_id": 0, "has_side_effects": True} if comm else {}
    return pl.pallas_call(
        functools.partial(kernel, place, comm),
        out_shape=(
            jax.ShapeDtypeStruct((3, 4, 16), f32),
            jax.ShapeDtypeStruct((1024, 128), f32),
            jax.ShapeDtypeStruct((1024, 128), f32),
        ),
        in_specs=[hbm] * 8 + [vm] * (len(operands) - 8),
        out_specs=(vm, vm, vm),
        scratch_shapes=[
            pltpu.SMEM((16,), i32),
            pltpu.VMEM((3, 8, 8), f32),
            pltpu.VMEM((8, 8), f32),
            pltpu.VMEM((8, 128), i32),
            pltpu.SMEM((4,), f32),
            pltpu.VMEM((32, 128), i32),
            pltpu.VMEM((32, 128), f32),
            pltpu.VMEM((3, 1024, 128), f32),
            pltpu.VMEM((2, 18, 4, 128), f32),
            pltpu.VMEM((1280, 256), bf16),
            pltpu.VMEM((512, 256), bf16),
            pltpu.VMEM((256, 256), bf16),
            pltpu.VMEM((576, 128), i32),
            pltpu.VMEM((576, 128), f32),
            pltpu.VMEM((9, 576, 128), bf16),
            plane(f32, 128),
            plane(f32, 128),
            plane(f32, 128),
            plane(bf16, 256),
            plane(bf16, 256),
            plane(bf16, 256),
            plane(bf16, 256),
            plane(bf16, 256),
            plane(bf16, 256),
            pltpu.VMEM((6, 256, 256), bf16),
            pltpu.VMEM((3, 4, 256, 128), f32),
            pltpu.VMEM((528, 384), bf16),
            pltpu.VMEM((480, 16), f32),
            pltpu.VMEM((8, 480, 128), f32),
            pltpu.VMEM((12, 8, 128), f32),
            pltpu.VMEM((2, 2, 128), f32),
            pltpu.VMEM((2, 15, 2, 128), f32),
            dma((8,)),
            dma,
            dma((2,)),
            dma((3,)),
            dma((3,)),
            dma((2,)),
            dma((2,)),
        ],
        compiler_params=pltpu.CompilerParams(vmem_limit_bytes=48 * 1024 * 1024, **extra),
        name="chain",
    )(*[pltpu.with_memory_space_constraint(a, pltpu.HBM) for a in operands[:8]], *operands[8:])


def copy_kernel(a_ref, b_ref, c_ref, a_out, b_out, c_out, sems):
    copies = []
    for k, (src, dst) in enumerate(((b_ref, b_out), (c_ref, c_out), (a_ref, a_out))):
        copies.append(pltpu.make_async_copy(src, dst, sems.at[k]))
        copies[-1].start()
    for copy in copies:
        copy.wait()


def copied(*arrays):
    return pl.pallas_call(
        copy_kernel,
        out_shape=[jax.ShapeDtypeStruct(a.shape, a.dtype) for a in arrays],
        in_specs=[pl.BlockSpec(memory_space=pltpu.VMEM)] * 3,
        out_specs=[pl.BlockSpec(memory_space=pltpu.HBM)] * 3,
        scratch_shapes=[pltpu.SemaphoreType.DMA((3,))],
        compiler_params=pltpu.CompilerParams(vmem_limit_bytes=48 * 1024 * 1024),
        name="copied",
    )(*arrays)


def where_am_i():
    tile = lax.axis_index("xy")
    return lax.axis_index("gz"), tile // 8, tile % 8


def per_device(
    left_vectors,
    sign_seeds,
    level_codes,
    level_table,
    disorder_sites,
    disorder_strength,
    hoppings,
    mass_raw,
):
    moments, prev, last = whole(
        where_am_i,
        True,
        sign_seeds,
        hoppings,
        mass_raw,
        level_codes.reshape(8, 128),
        level_table,
        disorder_sites.reshape(32, 128),
        disorder_strength.reshape(32, 128),
        left_vectors.reshape(3, 1024, 128),
    )
    moments, prev, last = copied(moments, prev, last)
    shape = left_vectors.shape[1:]
    return moments, prev.reshape(shape), last.reshape(shape)


def solution(mesh):
    in_specs = (
        P(None, None, None, "gz", "xy", None),
        P(),
        P("gz", "xy", None),
        P(),
        P(),
        P(),
        P(),
        P(),
    )
    out_specs = (P(), P(None, None, "gz", "xy", None), P(None, None, "gz", "xy", None))
    return jax.shard_map(
        per_device, mesh=mesh, in_specs=in_specs, out_specs=out_specs, check_vma=False
    )
```

```python
import functools
import math

import jax
import jax.numpy as jnp
from jax import lax
from jax.experimental import pallas as pl
from jax.experimental.pallas import tpu as pltpu
from jax.sharding import PartitionSpec as P

f32, bf16, i32 = jnp.float32, jnp.bfloat16, jnp.int32

PITCH = 24
NR = 608
LOHI = {0: (112, 496), 1: (80, 512), 2: (64, 544), 3: (32, 560)}
MULT = 668265261
NT = (((1,), (1,)), ((), ()))
highest = lax.Precision.HIGHEST


def split2(v):
    hi = v.astype(bf16)
    lo = (v - hi.astype(f32)).astype(bf16)
    return hi, lo


def split3(v):
    hi = v.astype(bf16)
    rest = v - hi.astype(f32)
    mid = rest.astype(bf16)
    lo = (rest - mid.astype(f32)).astype(bf16)
    return hi, mid, lo


def iota(shape, dim):
    return lax.broadcasted_iota(i32, shape, dim)


def rows_to_xy(rows):
    i = rows - 12
    q = lax.shift_right_arithmetic(i * 2731, jnp.full(i.shape, 16, i32))
    return q - 4, i - q * 24 - 4


def own_rows(block, lo):
    return jnp.concatenate(
        [block[112 + 24 * x - lo : 112 + 24 * x - lo + 16] for x in range(16)], axis=0
    )


def wrap32(value):
    value &= 0xFFFFFFFF
    return value - (1 << 32) if value >= (1 << 31) else value


def rows(parts):
    return jnp.concatenate(parts, axis=0)


def lanes_of(parts):
    return jnp.concatenate(parts, axis=1)


MESH = pl.DeviceIdType.MESH
SEGMENTS = ((0, 0, 96, 304), (0, 1, 288, 496), (-1, 1, 64, 112), (1, 0, 480, 544))


def kernel(
    place,
    comm,
    seed_hbm,
    hop_hbm,
    mass_hbm,
    codes_hbm,
    table_hbm,
    sites_hbm,
    strength_hbm,
    left_hbm,
    *refs,
):
    if not comm:
        (halo_in, a1_in, a2_in, c_in), refs = refs[:4], refs[4:]
    (
        moments_ref,
        prev_ref,
        last_ref,
        seed_ref,
        hop_ref,
        mass_ref,
        codes_ref,
        table_ref,
        sites_ref,
        strength_ref,
        left_ref,
        halo_ref,
        wm_ref,
        wy_ref,
        w0_ref,
            hb_ref,
        mk_ref,
        sb_ref,
        f0_ref,
        f1_ref,
        f2_ref,
        a0_ref,
        a1_ref,
        a2_ref,
        b0_ref,
        b1_ref,
        b2_ref,
        c_ref,
        lt_ref,
        sel_ref,
        obc_ref,
        ob_ref,
        acc_ref,
        part_ref,
        got_ref,
        load_sem,
        send_sem,
        recv_sem,
        pair_send_sem,
        pair_recv_sem,
        send2_sem,
        recv2_sem,
    ) = refs
    gz, tx, ty = place()
    odd = gz % 2 == 1
    flip = gz % 2 * 2 - 1

    def z_of(p):
        return (3 * (1 - gz % 2)) + flip * (p - 1)

    def await_copies(whole_ref, sem):
        pltpu.make_async_copy(whole_ref, whole_ref, sem).wait()

    if comm:
        near = [(dx, dy) for dx in (-1, 0, 1) for dy in (-1, 0, 1) if (dx, dy) != (0, 0)]
        outer = (gz + flip + 4) % 4
        inner = (gz - flip + 4) % 4
        tile = tx * 8 + ty
        column = tile // 4

        def neighbour(dx, dy, z):
            return {"gz": z, "xy": ((tx + dx + 8) % 8) * 8 + (ty + dy + 8) % 8}

        height = gz // 2 * 4 + tile % 4
        ring = sorted(range(1, 16), key=lambda k: -min(k // 2, 8 - k // 2))
        square = sorted(range(1, 16), key=lambda k: -min(k // 4, 4 - k // 4) - min(k % 4, 4 - k % 4))

        def along_z(step):
            k = ring[step - 1]
            high = (height + k // 2) % 8
            return {"gz": high // 4 * 2 + (gz + k) % 2, "xy": column * 4 + high % 4}

        def along_plane(step):
            k = square[step - 1]
            y, x = (column // 4 + k // 4) % 4, (column + k) % 4
            return {"gz": gz, "xy": (y * 4 + x) * 4 + tile % 4}

        barrier = pltpu.get_barrier_semaphore()
        partners = [neighbour(dx, dy, outer) for dx, dy in near]
        partners += [neighbour(dx, dy, gz) for dx, dy in near]
        partners += [f(step) for f in (along_z, along_plane) for step in range(1, 16)]
        for device in partners:
            pl.semaphore_signal(barrier, inc=1, device_id=device, device_id_type=MESH)

    loads = []
    for k, (src, dst) in enumerate(
        (
            (sites_hbm, sites_ref),
            (strength_hbm, strength_ref),
            (codes_hbm, codes_ref),
            (table_hbm, table_ref),
            (hop_hbm, hop_ref),
            (mass_hbm, mass_ref),
            (seed_hbm, seed_ref),
            (left_hbm, left_ref),
        )
    ):
        loads.append(pltpu.make_async_copy(src, dst, load_sem.at[k]))
        loads[-1].start()

    for load in loads[:4]:
        load.wait()
    codes = codes_ref[...]
    base = jnp.zeros((8, 128), f32)
    for level in range(4):
        base = jnp.where(codes == level, table_ref[level], base)
    site = sites_ref[...]
    lz = (site >> 14) - gz * 4
    lx = ((site >> 7) & 127) - tx * 16
    ly = (site & 127) - ty * 16
    inside = (lz >= 0) & (lz < 4) & (lx >= 0) & (lx < 16) & (ly >= 0) & (ly < 16)
    row = jnp.where(inside, lz * 2 + (lx >> 3), -1)
    col = (lx & 7) * 16 + ly
    pieces = split3(strength_ref[...])
    lhs, rhs = [], []
    for k in range(32):
        hit = jnp.broadcast_to(row[k : k + 1], (8, 128)) == iota((8, 128), 0)
        lhs.append(
            rows(
                [jnp.where(hit, jnp.broadcast_to(p[k : k + 1].astype(f32), (8, 128)), 0.0) for p in pieces]
                + [jnp.zeros((8, 128), f32)]
            ).astype(bf16)
        )
        at = jnp.broadcast_to(col[k : k + 1], (128, 128)) == iota((128, 128), 0)
        rhs.append(jnp.where(at, 1.0, 0.0).astype(bf16))
    added = lax.dot_general(lanes_of(lhs), lanes_of(rhs), NT, preferred_element_type=f32)
    onsite = base + (added[0:8] + added[8:16] + added[16:24])
    for h in range(2):
        up = [onsite[2 * z + h : 2 * z + h + 1] for z in range(4)]
        block = jnp.where(odd, rows(up), rows(up[::-1]))
        halo_ref[0, 8 + h] = block

    for load in loads[4:7]:
        load.wait()
    spread = jnp.where(iota((8, 128), 1) >> 4 == iota((8, 128), 0), 1.0, 0.0)
    mass_raw = mass_ref[...]
    mats = [0.5 * (mass_raw + mass_raw.T)]
    for d in range(3):
        mats += [hop_ref[d].T, hop_ref[d]]
    wide = jnp.dot(rows(mats) * 0.4, spread, precision=highest, preferred_element_type=f32)
    wide = [wide[8 * k : 8 * k + 8] for k in range(7)]
    same_r = (iota((16, 128), 1) & 15) == iota((16, 128), 0)

    def matrix(narrow):
        blocks = [jnp.where(same_r, jnp.broadcast_to(narrow[b : b + 1], (16, 128)), 0.0) for b in range(8)]
        return split2(rows(blocks))

    w_mass, w_xp, w_xm, w_yp, w_ym = [matrix(w) for w in wide[:5]]
    w_next = matrix(jnp.where(odd, wide[5], wide[6]))
    w_before = matrix(jnp.where(odd, wide[6], wide[5]))
    for slot, pair in enumerate((w_mass, w_xp, w_xm, w_next, w_before)):
        both = lanes_of(pair)
        wm_ref[256 * slot : 256 * slot + 128] = both
        wm_ref[256 * slot + 128 : 256 * slot + 256] = both
    for part in range(2):
        both = lanes_of([w_yp[part], w_ym[part]])
        wy_ref[256 * part : 256 * part + 128] = both
        wy_ref[256 * part + 128 : 256 * part + 256] = both
    w0_ref[0:128] = lanes_of(w_xp)
    w0_ref[128:256] = -lanes_of(w_xm)

    x, y = rows_to_xy(iota((576, 128), 0) + 8)
    lane = iota((576, 128), 1)
    xg = (tx * 16 + x + 128) & 127
    yg = ty * 16 + y
    lane1 = iota((1, 128), 1) & 15
    seeds = jnp.zeros((1, 128), i32)
    for r in range(16):
        seeds = jnp.where(lane1 == r, seed_ref[r], seeds)
    hb_ref[...] = ((xg * 128 + yg) * 8 + (lane >> 4)) * MULT + seeds
    mk_ref[...] = jnp.where((yg >= 0) & (yg < 128), 1.0, 0.0)

    def sign_plane(p, carry):
        zg = (gz * 4 + z_of(p) + 16) & 15
        word = hb_ref[...] + zg * wrap32(128 * 128 * 8 * MULT)
        word = word ^ lax.shift_right_logical(word, jnp.full(word.shape, 15, i32))
        word = word * -2048144789
        word = word ^ lax.shift_right_logical(word, jnp.full(word.shape, 13, i32))
        word = word * -1028477387
        mk = mk_ref[...]
        sb_ref[p] = jnp.where(word < 0, -mk, mk).astype(bf16)
        return carry

    lax.fori_loop(0, 9, sign_plane, 0)

    at = 0
    for dx, h, lo, hi in SEGMENTS:
        xr, yr = rows_to_xy(iota((hi - lo, 128), 0) + lo)
        xr = xr - 16 * dx - 8 * h
        ok = (xr >= 0) & (xr < 8)
        lane = iota((hi - lo, 128), 1)
        sels = []
        for dy in (-1, 0, 1):
            yy = yr - 16 * dy
            hit = ok & (yy >= 0) & (yy < 16) & (xr * 16 + yy == lane)
            sels.append(jnp.where(hit, 1.0, 0.0).astype(bf16))
        sel_ref[at : at + hi - lo] = lanes_of(sels)
        at += hi - lo

    fs = (f0_ref, f1_ref, f2_ref)
    as_ = (a0_ref, a1_ref, a2_ref)
    bs = (b0_ref, b1_ref, b2_ref)

    def keep(level, p, out, lo, hi):
        hi_f = out.astype(bf16).astype(f32)
        both = lanes_of([hi_f, out - hi_f])
        as_[level][p, lo:hi] = both.astype(bf16)
        bs[level][p, lo - 16 : hi] = rows([both[:8], both, both[:8]]).astype(bf16)

    def start(planes):
        lhs = []
        for p, radius in planes:
            lo, hi = LOHI[radius]
            lhs.append(lanes_of([sb_ref[p, lo + 16 : hi + 16], sb_ref[p, lo - 32 : hi - 32]]))
        prod = jnp.dot(rows(lhs), w0_ref[...], preferred_element_type=f32)
        prod = (prod[:, :128] + prod[:, 128:]) * 2.5
        at = 0
        for p, radius in planes:
            lo, hi = LOHI[radius]
            out = prod[at : at + hi - lo]
            at += hi - lo
            f0_ref[p, lo:hi] = out
            keep(0, p, out, lo, hi)

    start(((0, 2), (1, 3), (2, 3)))
    if comm:
        pl.semaphore_wait(barrier, len(partners))
        for dx, dy, far in (
            [(dx, dy, True) for dx, dy in near] + [(0, 0, True)] + [(dx, dy, False) for dx, dy in near]
        ):
            first, count = (1 if dx > 0 else 0, 1) if dx else (0, 2)
            there = 2 * ((1 - dx) * 3 + 1 - dy) + first
            pltpu.make_async_remote_copy(
                src_ref=halo_ref.at[0, pl.ds(8 + first, count)],
                dst_ref=halo_ref.at[int(far), pl.ds(there, count)],
                send_sem=send_sem,
                recv_sem=recv_sem.at[int(far)],
                device_id=neighbour(dx, dy, outer if far else gz),
                device_id_type=MESH,
            ).start()

    start(((3, 3), (4, 3), (5, 3)))
    start(((6, 2), (7, 1), (8, 0)))

    loads[7].wait()

    def turn_left(p, carry):
        for m in range(3):
            for h in range(2):
                lt_ref[m, p - 1, 128 * h : 128 * h + 128] = left_ref[m, pl.ds(2 * z_of(p) + h, 128, stride=8), :].T
        return carry

    lax.fori_loop(1, 5, turn_left, 0)
    acc_ref[...] = jnp.zeros(acc_ref.shape, f32)

    def halves(both):
        return both[:, :128] + both[:, 128:]

    def add_moments(n, p, velocity):
        for m in range(3):
            prod = lt_ref[m, p - 1] * velocity
            tot = prod[0:8]
            for k in range(8, 256, 8):
                tot = tot + prod[k : k + 8]
            acc_ref[m * 4 + n] += tot

    def hop(n, planes):
        a_ref, b_ref = as_[n], bs[n]
        lhs, nxt, before, ylhs = [], [], [], []
        for p, radius in planes:
            lo, hi = LOHI[radius]
            lhs.append(lanes_of([a_ref[p, lo:hi], b_ref[p, lo + 16 : hi + 16], b_ref[p, lo - 32 : hi - 32]]))
            nxt.append(a_ref[p + 1, lo:hi])
            before.append(a_ref[p - 1, lo:hi])
            first = 0 if radius == 1 else 16
            ylhs.append(a_ref[p, lo - first : hi + 16 - first])
        own = planes[0][0] <= 4
        if own:
            main = halves(jnp.dot(rows(lhs), wm_ref[0:768], preferred_element_type=f32))
            nxt = halves(jnp.dot(rows(nxt), wm_ref[768:1024], preferred_element_type=f32))
            before = halves(jnp.dot(rows(before), wm_ref[1024:1280], preferred_element_type=f32))
        else:
            all_lhs = lanes_of([rows(lhs), rows(nxt), rows(before)])
            main = halves(jnp.dot(all_lhs, wm_ref[...], preferred_element_type=f32))
        ylhs = rows(ylhs)
        yy = jnp.dot(lanes_of([ylhs, ylhs]), wy_ref[...], preferred_element_type=f32)
        yp = pltpu.roll(yy[:, :128], yy.shape[0] - 1, 0)
        ym = pltpu.roll(yy[:, 128:], 1, 0)
        outs, r, s = [], 0, 0
        for p, radius in planes:
            lo, hi = LOHI[radius]
            first = 0 if radius == 1 else 16
            size, t = hi - lo, s + first
            out = main[r : r + size] + yp[t : t + size] + ym[t : t + size]
            if own:
                up, down = nxt[r : r + size], before[r : r + size]
                out = out + up + down
                if p <= 4:
                    add_moments(n, p, own_rows(up, lo) - own_rows(down, lo))
            outs.append(out)
            r += size
            s += size + 16
        return outs

    def first_hop(planes):
        for (p, radius), out in zip(planes, hop(0, planes)):
            lo, hi = LOHI[radius]
            f1_ref[p, lo:hi] = out

    first_hop(((1, 2), (2, 2), (3, 2), (4, 2)))
    first_hop(((5, 2), (6, 1), (7, 0)))

    def energies(far, planes):
        obc_ref[...] = jnp.zeros(obc_ref.shape, f32)
        at = 0
        for dx, h, lo, hi in SEGMENTS:
            sels, vals = [], []
            for dy in (-1, 0, 1):
                sel = sel_ref[at : at + hi - lo, 128 * (dy + 1) : 128 * (dy + 2)]
                block = halo_ref[far, 2 * ((dx + 1) * 3 + dy + 1) + h]
                for piece in split3(rows([block, jnp.zeros((12, 128), f32)])):
                    sels.append(sel)
                    vals.append(piece)
            at += hi - lo
            obc_ref[lo - 64 : hi - 64] += lax.dot_general(
                lanes_of(sels), lanes_of(vals), NT, preferred_element_type=f32
            )
        spread_energies(planes)

    def spread_energies(planes):
        for p, col in planes:
            ob_ref[p] = jnp.broadcast_to(obc_ref[:, col : col + 1] * 0.4, (480, 128))

    def site_term(n, p, lo, hi):
        return ob_ref[p, lo - 64 : hi - 64] * fs[n][p, lo:hi]

    def first_rest(planes):
        for p, radius in planes:
            lo, hi = LOHI[radius]
            out = (f1_ref[p, lo:hi] + site_term(0, p, lo, hi)) * (mk_ref[lo - 8 : hi - 8] * 0.5)
            f1_ref[p, lo:hi] = out
            keep(1, p, out, lo, hi)

    def step(n, planes):
        for (p, radius), out in zip(planes, hop(n, planes)):
            lo, hi = LOHI[radius]
            out = (out + site_term(n, p, lo, hi)) * mk_ref[lo - 8 : hi - 8] - fs[n - 1][p, lo:hi]
            if n == 1:
                f2_ref[p, lo:hi] = out
                keep(2, p, out, lo, hi)
            else:
                v = own_rows(out, lo)
                hi_f = v.astype(bf16).astype(f32)
                c_ref[p] = lanes_of([hi_f, v - hi_f]).astype(bf16)
                f0_ref[p, 0:256] = v

    pair_sends = []

    def to_pair(level):
        if not comm:
            if level < 3:
                as_[level][0] = (a1_in, a2_in)[level - 1][...]
            else:
                c_ref[0] = c_in[2]
            return
        if level < 3:
            lo, hi = LOHI[2 - level]
            face = as_[level].at[:, pl.ds(lo, hi - lo)]
        else:
            face = c_ref
        pair_sends.append(
            pltpu.make_async_remote_copy(
                src_ref=face.at[1],
                dst_ref=face.at[0],
                send_sem=pair_send_sem.at[level - 1],
                recv_sem=pair_recv_sem.at[level - 1],
                device_id={"gz": inner, "xy": tile},
                device_id_type=MESH,
            )
        )
        pair_sends[-1].start()

    def from_pair():
        for send in pair_sends:
            send.wait()
        del pair_sends[:]

    if comm:
        await_copies(halo_ref.at[0, pl.ds(0, 10)], recv_sem.at[0])
    else:
        halo_ref[...] = halo_in[...]
    energies(0, [(1, 0)])
    first_rest(((1, 2),))
    to_pair(1)
    spread_energies([(p, p - 1) for p in range(2, 5)])
    first_rest(((2, 2), (3, 2), (4, 2)))
    step(1, ((2, 1), (3, 1)))
    from_pair()
    step(1, ((1, 1),))
    to_pair(2)
    if comm:
        await_copies(halo_ref.at[1, pl.ds(0, 12)], recv_sem.at[1])
    energies(1, [(p, 8 - p) for p in range(5, 8)])
    first_rest(((5, 2), (6, 1), (7, 0)))
    step(1, ((4, 1), (5, 1), (6, 0)))
    step(2, ((2, 0), (3, 0)))
    from_pair()
    step(2, ((1, 0),))
    to_pair(3)
    step(2, ((4, 0), (5, 0)))

    def z_product(slot, planes):
        lhs = rows([c_ref[p] for p in planes])
        return halves(jnp.dot(lhs, wm_ref[256 * slot : 256 * slot + 256], preferred_element_type=f32))

    nxt = z_product(3, (2, 3, 4, 5))
    before = z_product(4, (1, 2, 3))
    for p in (2, 3, 4):
        add_moments(3, p, nxt[256 * p - 256 : 256 * p] - before[256 * p - 512 : 256 * p - 256])
    from_pair()
    add_moments(3, 1, nxt[:256] - z_product(4, (0,)))

    fold = jnp.where((iota((128, 128), 0) & 15) == (iota((128, 128), 1) & 15), 1.0, 0.0)
    folded = jnp.dot(acc_ref[...].reshape(96, 128), fold, precision=highest, preferred_element_type=f32)
    mine = (iota((96, 128), 1) >> 4) == ((iota((96, 128), 0) >> 3) & 7)
    folded = jnp.where(mine, folded, 0.0) * (flip.astype(f32) * (2.5 / math.sqrt(8 * 262144)))
    part = rows([jnp.sum(folded[:64], axis=0, keepdims=True), jnp.sum(folded[64:], axis=0, keepdims=True)])
    part_ref[0] = part

    def send_part(stage, target):
        for step in range(1, 16):
            pltpu.make_async_remote_copy(
                src_ref=part_ref.at[stage],
                dst_ref=got_ref.at[stage, step - 1],
                send_sem=send2_sem.at[stage],
                recv_sem=recv2_sem.at[stage],
                device_id=target(step),
                device_id_type=MESH,
            ).start()

    def add_parts(stage, total):
        await_copies(got_ref.at[stage], recv2_sem.at[stage])
        return total + jnp.sum(got_ref[stage], axis=0)

    if comm:
        send_part(0, along_z)

    def plane_out(p, carry):
        last = f0_ref[p, 0:256].T
        prev = own_rows(f2_ref[p, 80:512], 80).T
        for h in range(2):
            place_of = pl.ds(2 * z_of(p) + h, 128, stride=8)
            last_ref[place_of, :] = last[:, 128 * h : 128 * h + 128]
            prev_ref[place_of, :] = prev[:, 128 * h : 128 * h + 128]
        return carry

    lax.fori_loop(1, 5, plane_out, 0)

    if comm:
        part = add_parts(0, part)
        part_ref[1] = part
        send_part(1, along_plane)
        part = add_parts(1, part)
        await_copies(halo_ref.at[0, pl.ds(0, 10)], send_sem)
        await_copies(halo_ref.at[1, pl.ds(0, 12)], send_sem)
        await_copies(got_ref.at[0], send2_sem.at[0])
        await_copies(got_ref.at[1], send2_sem.at[1])
    for k in range(12):
        moments_ref[k // 4, k % 4 : k % 4 + 1, :] = part[k // 8 : k // 8 + 1, 16 * (k % 8) : 16 * (k % 8) + 16]


def whole(place, comm, *operands):
    hbm = pl.BlockSpec(memory_space=pltpu.HBM)
    vm = pl.BlockSpec(memory_space=pltpu.VMEM)
    plane = lambda kind, lanes: pltpu.VMEM((9, NR, lanes), kind)
    dma = pltpu.SemaphoreType.DMA
    extra = {"collective_id": 0, "has_side_effects": True} if comm else {}
    return pl.pallas_call(
        functools.partial(kernel, place, comm),
        out_shape=(
            jax.ShapeDtypeStruct((3, 4, 16), f32),
            jax.ShapeDtypeStruct((1024, 128), f32),
            jax.ShapeDtypeStruct((1024, 128), f32),
        ),
        in_specs=[hbm] * 8 + [vm] * (len(operands) - 8),
        out_specs=(vm, vm, vm),
        scratch_shapes=[
            pltpu.SMEM((16,), i32),
            pltpu.VMEM((3, 8, 8), f32),
            pltpu.VMEM((8, 8), f32),
            pltpu.VMEM((8, 128), i32),
            pltpu.SMEM((4,), f32),
            pltpu.VMEM((32, 128), i32),
            pltpu.VMEM((32, 128), f32),
            pltpu.VMEM((3, 1024, 128), f32),
            pltpu.VMEM((2, 18, 4, 128), f32),
            pltpu.VMEM((1280, 256), bf16),
            pltpu.VMEM((512, 256), bf16),
            pltpu.VMEM((256, 256), bf16),
            pltpu.VMEM((576, 128), i32),
            pltpu.VMEM((576, 128), f32),
            pltpu.VMEM((9, 576, 128), bf16),
            plane(f32, 128),
            plane(f32, 128),
            plane(f32, 128),
            plane(bf16, 256),
            plane(bf16, 256),
            plane(bf16, 256),
            plane(bf16, 256),
            plane(bf16, 256),
            plane(bf16, 256),
            pltpu.VMEM((6, 256, 256), bf16),
            pltpu.VMEM((3, 4, 256, 128), f32),
            pltpu.VMEM((528, 384), bf16),
            pltpu.VMEM((480, 16), f32),
            pltpu.VMEM((8, 480, 128), f32),
            pltpu.VMEM((12, 8, 128), f32),
            pltpu.VMEM((2, 2, 128), f32),
            pltpu.VMEM((2, 15, 2, 128), f32),
            dma((8,)),
            dma,
            dma((2,)),
            dma((3,)),
            dma((3,)),
            dma((2,)),
            dma((2,)),
        ],
        compiler_params=pltpu.CompilerParams(vmem_limit_bytes=48 * 1024 * 1024, **extra),
        name="chain",
    )(*[pltpu.with_memory_space_constraint(a, pltpu.HBM) for a in operands[:8]], *operands[8:])


def copy_kernel(a_ref, b_ref, c_ref, a_out, b_out, c_out, sems):
    copies = []
    for k, (src, dst) in enumerate(((b_ref, b_out), (c_ref, c_out), (a_ref, a_out))):
        copies.append(pltpu.make_async_copy(src, dst, sems.at[k]))
        copies[-1].start()
    for copy in copies:
        copy.wait()


def copied(*arrays):
    return pl.pallas_call(
        copy_kernel,
        out_shape=[jax.ShapeDtypeStruct(a.shape, a.dtype) for a in arrays],
        in_specs=[pl.BlockSpec(memory_space=pltpu.VMEM)] * 3,
        out_specs=[pl.BlockSpec(memory_space=pltpu.HBM)] * 3,
        scratch_shapes=[pltpu.SemaphoreType.DMA((3,))],
        compiler_params=pltpu.CompilerParams(vmem_limit_bytes=48 * 1024 * 1024),
        name="copied",
    )(*arrays)


def where_am_i():
    tile = lax.axis_index("xy")
    return lax.axis_index("gz"), tile // 8, tile % 8


def per_device(
    left_vectors,
    sign_seeds,
    level_codes,
    level_table,
    disorder_sites,
    disorder_strength,
    hoppings,
    mass_raw,
):
    moments, prev, last = whole(
        where_am_i,
        True,
        sign_seeds,
        hoppings,
        mass_raw,
        level_codes.reshape(8, 128),
        level_table,
        disorder_sites.reshape(32, 128),
        disorder_strength.reshape(32, 128),
        left_vectors.reshape(3, 1024, 128),
    )
    moments, prev, last = copied(moments, prev, last)
    shape = left_vectors.shape[1:]
    return moments, prev.reshape(shape), last.reshape(shape)


def solution(mesh):
    in_specs = (
        P(None, None, None, "gz", "xy", None),
        P(),
        P("gz", "xy", None),
        P(),
        P(),
        P(),
        P(),
        P(),
    )
    out_specs = (P(), P(None, None, "gz", "xy", None), P(None, None, "gz", "xy", None))
    return jax.shard_map(
        per_device, mesh=mesh, in_specs=in_specs, out_specs=out_specs, check_vma=False
    )
```

```python
import functools
import math

import jax
import jax.numpy as jnp
from jax import lax
from jax.experimental import pallas as pl
from jax.experimental.pallas import tpu as pltpu
from jax.sharding import PartitionSpec as P

f32, bf16, i32 = jnp.float32, jnp.bfloat16, jnp.int32

PITCH = 24
NR = 608
LOHI = {0: (112, 496), 1: (80, 512), 2: (64, 544), 3: (32, 560)}
MULT = 668265261
NT = (((1,), (1,)), ((), ()))
highest = lax.Precision.HIGHEST


def split2(v):
    hi = v.astype(bf16)
    lo = (v - hi.astype(f32)).astype(bf16)
    return hi, lo


def split3(v):
    hi = v.astype(bf16)
    rest = v - hi.astype(f32)
    mid = rest.astype(bf16)
    lo = (rest - mid.astype(f32)).astype(bf16)
    return hi, mid, lo


def iota(shape, dim):
    return lax.broadcasted_iota(i32, shape, dim)


def rows_to_xy(rows):
    i = rows - 12
    q = lax.shift_right_arithmetic(i * 2731, jnp.full(i.shape, 16, i32))
    return q - 4, i - q * 24 - 4


def own_rows(block, lo):
    return jnp.concatenate(
        [block[112 + 24 * x - lo : 112 + 24 * x - lo + 16] for x in range(16)], axis=0
    )


def wrap32(value):
    value &= 0xFFFFFFFF
    return value - (1 << 32) if value >= (1 << 31) else value


def rows(parts):
    return jnp.concatenate(parts, axis=0)


def lanes_of(parts):
    return jnp.concatenate(parts, axis=1)


MESH = pl.DeviceIdType.MESH
SEGMENTS = ((0, 0, 96, 304), (0, 1, 288, 496), (-1, 1, 64, 112), (1, 0, 480, 544))


def kernel(
    place,
    comm,
    seed_hbm,
    hop_hbm,
    mass_hbm,
    codes_hbm,
    table_hbm,
    sites_hbm,
    strength_hbm,
    left_hbm,
    *refs,
):
    if not comm:
        (halo_in, a1_in, a2_in, c_in), refs = refs[:4], refs[4:]
    (
        moments_ref,
        prev_ref,
        last_ref,
        seed_ref,
        hop_ref,
        mass_ref,
        codes_ref,
        table_ref,
        sites_ref,
        strength_ref,
        left_ref,
        halo_ref,
        wm_ref,
        wy_ref,
        w0_ref,
            hb_ref,
        mk_ref,
        sb_ref,
        f0_ref,
        f1_ref,
        f2_ref,
        a0_ref,
        a1_ref,
        a2_ref,
        b0_ref,
        b1_ref,
        b2_ref,
        c_ref,
        lt_ref,
        sel_ref,
        obc_ref,
        ob_ref,
        acc_ref,
        part_ref,
        got_ref,
        load_sem,
        send_sem,
        recv_sem,
        pair_send_sem,
        pair_recv_sem,
        send2_sem,
        recv2_sem,
    ) = refs
    gz, tx, ty = place()
    odd = gz % 2 == 1
    flip = gz % 2 * 2 - 1

    def z_of(p):
        return (3 * (1 - gz % 2)) + flip * (p - 1)

    def await_copies(whole_ref, sem):
        pltpu.make_async_copy(whole_ref, whole_ref, sem).wait()

    if comm:
        near = [(dx, dy) for dx in (-1, 0, 1) for dy in (-1, 0, 1) if (dx, dy) != (0, 0)]
        outer = (gz + flip + 4) % 4
        inner = (gz - flip + 4) % 4
        tile = tx * 8 + ty
        column = tile // 4

        def neighbour(dx, dy, z):
            return {"gz": z, "xy": ((tx + dx + 8) % 8) * 8 + (ty + dy + 8) % 8}

        height = gz // 2 * 4 + tile % 4
        ring = sorted(range(1, 16), key=lambda k: -min(k // 2, 8 - k // 2))
        square = sorted(range(1, 16), key=lambda k: -min(k // 4, 4 - k // 4) - min(k % 4, 4 - k % 4))

        def along_z(step):
            k = ring[step - 1]
            high = (height + k // 2) % 8
            return {"gz": high // 4 * 2 + (gz + k) % 2, "xy": column * 4 + high % 4}

        def along_plane(step):
            k = square[step - 1]
            y, x = (column // 4 + k // 4) % 4, (column + k) % 4
            return {"gz": gz, "xy": (y * 4 + x) * 4 + tile % 4}

        barrier = pltpu.get_barrier_semaphore()
        partners = [neighbour(dx, dy, outer) for dx, dy in near]
        partners += [neighbour(dx, dy, gz) for dx, dy in near]
        partners += [f(step) for f in (along_z, along_plane) for step in range(1, 16)]
        for device in partners:
            pl.semaphore_signal(barrier, inc=1, device_id=device, device_id_type=MESH)

    loads = []
    for k, (src, dst) in enumerate(
        (
            (sites_hbm, sites_ref),
            (strength_hbm, strength_ref),
            (codes_hbm, codes_ref),
            (table_hbm, table_ref),
            (hop_hbm, hop_ref),
            (mass_hbm, mass_ref),
            (seed_hbm, seed_ref),
            (left_hbm, left_ref),
        )
    ):
        loads.append(pltpu.make_async_copy(src, dst, load_sem.at[k]))
        loads[-1].start()

    for load in loads[:4]:
        load.wait()
    codes = codes_ref[...]
    base = jnp.zeros((8, 128), f32)
    for level in range(4):
        base = jnp.where(codes == level, table_ref[level], base)
    site = sites_ref[...]
    lz = (site >> 14) - gz * 4
    lx = ((site >> 7) & 127) - tx * 16
    ly = (site & 127) - ty * 16
    inside = (lz >= 0) & (lz < 4) & (lx >= 0) & (lx < 16) & (ly >= 0) & (ly < 16)
    row = jnp.where(inside, lz * 2 + (lx >> 3), -1)
    col = (lx & 7) * 16 + ly
    pieces = split3(strength_ref[...])
    lhs, rhs = [], []
    for k in range(32):
        hit = jnp.broadcast_to(row[k : k + 1], (8, 128)) == iota((8, 128), 0)
        lhs.append(
            rows(
                [jnp.where(hit, jnp.broadcast_to(p[k : k + 1].astype(f32), (8, 128)), 0.0) for p in pieces]
                + [jnp.zeros((8, 128), f32)]
            ).astype(bf16)
        )
        at = jnp.broadcast_to(col[k : k + 1], (128, 128)) == iota((128, 128), 0)
        rhs.append(jnp.where(at, 1.0, 0.0).astype(bf16))
    added = lax.dot_general(lanes_of(lhs), lanes_of(rhs), NT, preferred_element_type=f32)
    onsite = base + (added[0:8] + added[8:16] + added[16:24])
    for h in range(2):
        up = [onsite[2 * z + h : 2 * z + h + 1] for z in range(4)]
        block = jnp.where(odd, rows(up), rows(up[::-1]))
        halo_ref[0, 8 + h] = block

    for load in loads[4:7]:
        load.wait()
    spread = jnp.where(iota((8, 128), 1) >> 4 == iota((8, 128), 0), 1.0, 0.0)
    mass_raw = mass_ref[...]
    mats = [0.5 * (mass_raw + mass_raw.T)]
    for d in range(3):
        mats += [hop_ref[d].T, hop_ref[d]]
    wide = jnp.dot(rows(mats) * 0.4, spread, precision=highest, preferred_element_type=f32)
    wide = [wide[8 * k : 8 * k + 8] for k in range(7)]
    same_r = (iota((16, 128), 1) & 15) == iota((16, 128), 0)

    def matrix(narrow):
        blocks = [jnp.where(same_r, jnp.broadcast_to(narrow[b : b + 1], (16, 128)), 0.0) for b in range(8)]
        return split2(rows(blocks))

    w_mass, w_xp, w_xm, w_yp, w_ym = [matrix(w) for w in wide[:5]]
    w_next = matrix(jnp.where(odd, wide[5], wide[6]))
    w_before = matrix(jnp.where(odd, wide[6], wide[5]))
    for slot, pair in enumerate((w_mass, w_xp, w_xm, w_next, w_before)):
        both = lanes_of(pair)
        wm_ref[256 * slot : 256 * slot + 128] = both
        wm_ref[256 * slot + 128 : 256 * slot + 256] = both
    for part in range(2):
        both = lanes_of([w_yp[part], w_ym[part]])
        wy_ref[256 * part : 256 * part + 128] = both
        wy_ref[256 * part + 128 : 256 * part + 256] = both
    w0_ref[0:128] = lanes_of(w_xp)
    w0_ref[128:256] = -lanes_of(w_xm)

    x, y = rows_to_xy(iota((576, 128), 0) + 8)
    lane = iota((576, 128), 1)
    xg = (tx * 16 + x + 128) & 127
    yg = ty * 16 + y
    lane1 = iota((1, 128), 1) & 15
    seeds = jnp.zeros((1, 128), i32)
    for r in range(16):
        seeds = jnp.where(lane1 == r, seed_ref[r], seeds)
    hb_ref[...] = ((xg * 128 + yg) * 8 + (lane >> 4)) * MULT + seeds
    mk_ref[...] = jnp.where((yg >= 0) & (yg < 128), 1.0, 0.0)

    def sign_plane(p, carry):
        zg = (gz * 4 + z_of(p) + 16) & 15
        word = hb_ref[...] + zg * wrap32(128 * 128 * 8 * MULT)
        word = word ^ lax.shift_right_logical(word, jnp.full(word.shape, 15, i32))
        word = word * -2048144789
        word = word ^ lax.shift_right_logical(word, jnp.full(word.shape, 13, i32))
        word = word * -1028477387
        mk = mk_ref[...]
        sb_ref[p] = jnp.where(word < 0, -mk, mk).astype(bf16)
        return carry

    lax.fori_loop(0, 9, sign_plane, 0)

    at = 0
    for dx, h, lo, hi in SEGMENTS:
        xr, yr = rows_to_xy(iota((hi - lo, 128), 0) + lo)
        xr = xr - 16 * dx - 8 * h
        ok = (xr >= 0) & (xr < 8)
        lane = iota((hi - lo, 128), 1)
        sels = []
        for dy in (-1, 0, 1):
            yy = yr - 16 * dy
            hit = ok & (yy >= 0) & (yy < 16) & (xr * 16 + yy == lane)
            sels.append(jnp.where(hit, 1.0, 0.0).astype(bf16))
        sel_ref[at : at + hi - lo] = lanes_of(sels)
        at += hi - lo

    fs = (f0_ref, f1_ref, f2_ref)
    as_ = (a0_ref, a1_ref, a2_ref)
    bs = (b0_ref, b1_ref, b2_ref)

    def keep(level, p, out, lo, hi):
        hi_f = out.astype(bf16).astype(f32)
        both = lanes_of([hi_f, out - hi_f])
        as_[level][p, lo:hi] = both.astype(bf16)
        bs[level][p, lo - 16 : hi] = rows([both[:8], both, both[:8]]).astype(bf16)

    def start(planes):
        lhs = []
        for p, radius in planes:
            lo, hi = LOHI[radius]
            lhs.append(lanes_of([sb_ref[p, lo + 16 : hi + 16], sb_ref[p, lo - 32 : hi - 32]]))
        prod = jnp.dot(rows(lhs), w0_ref[...], preferred_element_type=f32)
        prod = (prod[:, :128] + prod[:, 128:]) * 2.5
        at = 0
        for p, radius in planes:
            lo, hi = LOHI[radius]
            out = prod[at : at + hi - lo]
            at += hi - lo
            f0_ref[p, lo:hi] = out
            keep(0, p, out, lo, hi)

    start(((0, 2), (1, 3), (2, 3)))
    if comm:
        pl.semaphore_wait(barrier, len(partners))
        for dx, dy, far in (
            [(dx, dy, False) for dx, dy in near] + [(dx, dy, True) for dx, dy in near] + [(0, 0, True)]
        ):
            first, count = (1 if dx > 0 else 0, 1) if dx else (0, 2)
            there = 2 * ((1 - dx) * 3 + 1 - dy) + first
            pltpu.make_async_remote_copy(
                src_ref=halo_ref.at[0, pl.ds(8 + first, count)],
                dst_ref=halo_ref.at[int(far), pl.ds(there, count)],
                send_sem=send_sem,
                recv_sem=recv_sem.at[int(far)],
                device_id=neighbour(dx, dy, outer if far else gz),
                device_id_type=MESH,
            ).start()

    start(((3, 3), (4, 3), (5, 3)))
    start(((6, 2), (7, 1), (8, 0)))

    loads[7].wait()

    def turn_left(p, carry):
        for m in range(3):
            for h in range(2):
                lt_ref[m, p - 1, 128 * h : 128 * h + 128] = left_ref[m, pl.ds(2 * z_of(p) + h, 128, stride=8), :].T
        return carry

    lax.fori_loop(1, 5, turn_left, 0)
    acc_ref[...] = jnp.zeros(acc_ref.shape, f32)

    def halves(both):
        return both[:, :128] + both[:, 128:]

    def add_moments(n, p, velocity):
        for m in range(3):
            prod = lt_ref[m, p - 1] * velocity
            tot = prod[0:8]
            for k in range(8, 256, 8):
                tot = tot + prod[k : k + 8]
            acc_ref[m * 4 + n] += tot

    def hop(n, planes):
        a_ref, b_ref = as_[n], bs[n]
        lhs, nxt, before, ylhs = [], [], [], []
        for p, radius in planes:
            lo, hi = LOHI[radius]
            lhs.append(lanes_of([a_ref[p, lo:hi], b_ref[p, lo + 16 : hi + 16], b_ref[p, lo - 32 : hi - 32]]))
            nxt.append(a_ref[p + 1, lo:hi])
            before.append(a_ref[p - 1, lo:hi])
            first = 0 if radius == 1 else 16
            ylhs.append(a_ref[p, lo - first : hi + 16 - first])
        own = planes[0][0] <= 4
        if own:
            main = halves(jnp.dot(rows(lhs), wm_ref[0:768], preferred_element_type=f32))
            nxt = halves(jnp.dot(rows(nxt), wm_ref[768:1024], preferred_element_type=f32))
            before = halves(jnp.dot(rows(before), wm_ref[1024:1280], preferred_element_type=f32))
        else:
            all_lhs = lanes_of([rows(lhs), rows(nxt), rows(before)])
            main = halves(jnp.dot(all_lhs, wm_ref[...], preferred_element_type=f32))
        ylhs = rows(ylhs)
        yy = jnp.dot(lanes_of([ylhs, ylhs]), wy_ref[...], preferred_element_type=f32)
        yp = pltpu.roll(yy[:, :128], yy.shape[0] - 1, 0)
        ym = pltpu.roll(yy[:, 128:], 1, 0)
        outs, r, s = [], 0, 0
        for p, radius in planes:
            lo, hi = LOHI[radius]
            first = 0 if radius == 1 else 16
            size, t = hi - lo, s + first
            out = main[r : r + size] + yp[t : t + size] + ym[t : t + size]
            if own:
                up, down = nxt[r : r + size], before[r : r + size]
                out = out + up + down
                if p <= 4:
                    add_moments(n, p, own_rows(up, lo) - own_rows(down, lo))
            outs.append(out)
            r += size
            s += size + 16
        return outs

    def first_hop(planes):
        for (p, radius), out in zip(planes, hop(0, planes)):
            lo, hi = LOHI[radius]
            f1_ref[p, lo:hi] = out

    first_hop(((1, 2), (2, 2), (3, 2), (4, 2)))
    first_hop(((5, 2), (6, 1), (7, 0)))

    def energies(far, planes):
        obc_ref[...] = jnp.zeros(obc_ref.shape, f32)
        at = 0
        for dx, h, lo, hi in SEGMENTS:
            sels, vals = [], []
            for dy in (-1, 0, 1):
                sel = sel_ref[at : at + hi - lo, 128 * (dy + 1) : 128 * (dy + 2)]
                block = halo_ref[far, 2 * ((dx + 1) * 3 + dy + 1) + h]
                for piece in split3(rows([block, jnp.zeros((12, 128), f32)])):
                    sels.append(sel)
                    vals.append(piece)
            at += hi - lo
            obc_ref[lo - 64 : hi - 64] += lax.dot_general(
                lanes_of(sels), lanes_of(vals), NT, preferred_element_type=f32
            )
        spread_energies(planes)

    def spread_energies(planes):
        for p, col in planes:
            ob_ref[p] = jnp.broadcast_to(obc_ref[:, col : col + 1] * 0.4, (480, 128))

    def site_term(n, p, lo, hi):
        return ob_ref[p, lo - 64 : hi - 64] * fs[n][p, lo:hi]

    def first_rest(planes):
        for p, radius in planes:
            lo, hi = LOHI[radius]
            out = (f1_ref[p, lo:hi] + site_term(0, p, lo, hi)) * (mk_ref[lo - 8 : hi - 8] * 0.5)
            f1_ref[p, lo:hi] = out
            keep(1, p, out, lo, hi)

    def step(n, planes):
        for (p, radius), out in zip(planes, hop(n, planes)):
            lo, hi = LOHI[radius]
            out = (out + site_term(n, p, lo, hi)) * mk_ref[lo - 8 : hi - 8] - fs[n - 1][p, lo:hi]
            if n == 1:
                f2_ref[p, lo:hi] = out
                keep(2, p, out, lo, hi)
            else:
                v = own_rows(out, lo)
                hi_f = v.astype(bf16).astype(f32)
                c_ref[p] = lanes_of([hi_f, v - hi_f]).astype(bf16)
                f0_ref[p, 0:256] = v

    pair_sends = []

    def to_pair(level):
        if not comm:
            if level < 3:
                as_[level][0] = (a1_in, a2_in)[level - 1][...]
            else:
                c_ref[0] = c_in[2]
            return
        if level < 3:
            lo, hi = LOHI[2 - level]
            face = as_[level].at[:, pl.ds(lo, hi - lo)]
        else:
            face = c_ref
        pair_sends.append(
            pltpu.make_async_remote_copy(
                src_ref=face.at[1],
                dst_ref=face.at[0],
                send_sem=pair_send_sem.at[level - 1],
                recv_sem=pair_recv_sem.at[level - 1],
                device_id={"gz": inner, "xy": tile},
                device_id_type=MESH,
            )
        )
        pair_sends[-1].start()

    def from_pair():
        for send in pair_sends:
            send.wait()
        del pair_sends[:]

    if comm:
        await_copies(halo_ref.at[0, pl.ds(0, 10)], recv_sem.at[0])
    else:
        halo_ref[...] = halo_in[...]
    energies(0, [(1, 0)])
    first_rest(((1, 2),))
    to_pair(1)
    spread_energies([(p, p - 1) for p in range(2, 5)])
    first_rest(((2, 2), (3, 2), (4, 2)))
    step(1, ((2, 1), (3, 1)))
    from_pair()
    step(1, ((1, 1),))
    to_pair(2)
    if comm:
        await_copies(halo_ref.at[1, pl.ds(0, 12)], recv_sem.at[1])
    energies(1, [(p, 8 - p) for p in range(5, 8)])
    first_rest(((5, 2), (6, 1), (7, 0)))
    step(1, ((4, 1), (5, 1), (6, 0)))
    step(2, ((2, 0), (3, 0)))
    from_pair()
    step(2, ((1, 0),))
    to_pair(3)
    step(2, ((4, 0), (5, 0)))

    def z_product(slot, planes):
        lhs = rows([c_ref[p] for p in planes])
        return halves(jnp.dot(lhs, wm_ref[256 * slot : 256 * slot + 256], preferred_element_type=f32))

    nxt = z_product(3, (2, 3, 4, 5))
    before = z_product(4, (1, 2, 3))
    for p in (2, 3, 4):
        add_moments(3, p, nxt[256 * p - 256 : 256 * p] - before[256 * p - 512 : 256 * p - 256])
    from_pair()
    add_moments(3, 1, nxt[:256] - z_product(4, (0,)))

    fold = jnp.where((iota((128, 128), 0) & 15) == (iota((128, 128), 1) & 15), 1.0, 0.0)
    folded = jnp.dot(acc_ref[...].reshape(96, 128), fold, precision=highest, preferred_element_type=f32)
    mine = (iota((96, 128), 1) >> 4) == ((iota((96, 128), 0) >> 3) & 7)
    folded = jnp.where(mine, folded, 0.0) * (flip.astype(f32) * (2.5 / math.sqrt(8 * 262144)))
    part = rows([jnp.sum(folded[:64], axis=0, keepdims=True), jnp.sum(folded[64:], axis=0, keepdims=True)])
    part_ref[0] = part

    def send_part(stage, target):
        for step in range(1, 16):
            pltpu.make_async_remote_copy(
                src_ref=part_ref.at[stage],
                dst_ref=got_ref.at[stage, step - 1],
                send_sem=send2_sem.at[stage],
                recv_sem=recv2_sem.at[stage],
                device_id=target(step),
                device_id_type=MESH,
            ).start()

    def add_parts(stage, total):
        await_copies(got_ref.at[stage], recv2_sem.at[stage])
        return total + jnp.sum(got_ref[stage], axis=0)

    if comm:
        send_part(0, along_z)

    def plane_out(p, carry):
        last = f0_ref[p, 0:256].T
        prev = own_rows(f2_ref[p, 80:512], 80).T
        for h in range(2):
            place_of = pl.ds(2 * z_of(p) + h, 128, stride=8)
            last_ref[place_of, :] = last[:, 128 * h : 128 * h + 128]
            prev_ref[place_of, :] = prev[:, 128 * h : 128 * h + 128]
        return carry

    lax.fori_loop(1, 5, plane_out, 0)

    if comm:
        part = add_parts(0, part)
        part_ref[1] = part
        send_part(1, along_plane)
        part = add_parts(1, part)
        await_copies(halo_ref.at[0, pl.ds(0, 10)], send_sem)
        await_copies(halo_ref.at[1, pl.ds(0, 12)], send_sem)
        await_copies(got_ref.at[0], send2_sem.at[0])
        await_copies(got_ref.at[1], send2_sem.at[1])
    for k in range(12):
        moments_ref[k // 4, k % 4 : k % 4 + 1, :] = part[k // 8 : k // 8 + 1, 16 * (k % 8) : 16 * (k % 8) + 16]


def whole(place, comm, *operands):
    hbm = pl.BlockSpec(memory_space=pltpu.HBM)
    vm = pl.BlockSpec(memory_space=pltpu.VMEM)
    plane = lambda kind, lanes: pltpu.VMEM((9, NR, lanes), kind)
    dma = pltpu.SemaphoreType.DMA
    extra = {"collective_id": 0, "has_side_effects": True} if comm else {}
    return pl.pallas_call(
        functools.partial(kernel, place, comm),
        out_shape=(
            jax.ShapeDtypeStruct((3, 4, 16), f32),
            jax.ShapeDtypeStruct((1024, 128), f32),
            jax.ShapeDtypeStruct((1024, 128), f32),
        ),
        in_specs=[hbm] * 8 + [vm] * (len(operands) - 8),
        out_specs=(vm, vm, vm),
        scratch_shapes=[
            pltpu.SMEM((16,), i32),
            pltpu.VMEM((3, 8, 8), f32),
            pltpu.VMEM((8, 8), f32),
            pltpu.VMEM((8, 128), i32),
            pltpu.SMEM((4,), f32),
            pltpu.VMEM((32, 128), i32),
            pltpu.VMEM((32, 128), f32),
            pltpu.VMEM((3, 1024, 128), f32),
            pltpu.VMEM((2, 18, 4, 128), f32),
            pltpu.VMEM((1280, 256), bf16),
            pltpu.VMEM((512, 256), bf16),
            pltpu.VMEM((256, 256), bf16),
            pltpu.VMEM((576, 128), i32),
            pltpu.VMEM((576, 128), f32),
            pltpu.VMEM((9, 576, 128), bf16),
            plane(f32, 128),
            plane(f32, 128),
            plane(f32, 128),
            plane(bf16, 256),
            plane(bf16, 256),
            plane(bf16, 256),
            plane(bf16, 256),
            plane(bf16, 256),
            plane(bf16, 256),
            pltpu.VMEM((6, 256, 256), bf16),
            pltpu.VMEM((3, 4, 256, 128), f32),
            pltpu.VMEM((528, 384), bf16),
            pltpu.VMEM((480, 16), f32),
            pltpu.VMEM((8, 480, 128), f32),
            pltpu.VMEM((12, 8, 128), f32),
            pltpu.VMEM((2, 2, 128), f32),
            pltpu.VMEM((2, 15, 2, 128), f32),
            dma((8,)),
            dma,
            dma((2,)),
            dma((3,)),
            dma((3,)),
            dma((2,)),
            dma((2,)),
        ],
        compiler_params=pltpu.CompilerParams(vmem_limit_bytes=48 * 1024 * 1024, **extra),
        name="chain",
    )(*[pltpu.with_memory_space_constraint(a, pltpu.HBM) for a in operands[:8]], *operands[8:])


def copy_kernel(a_ref, b_ref, c_ref, a_out, b_out, c_out, sems):
    copies = []
    for k, (src, dst) in enumerate(((b_ref, b_out), (c_ref, c_out), (a_ref, a_out))):
        copies.append(pltpu.make_async_copy(src, dst, sems.at[k]))
        copies[-1].start()
    for copy in copies:
        copy.wait()


def copied(*arrays):
    return pl.pallas_call(
        copy_kernel,
        out_shape=[jax.ShapeDtypeStruct(a.shape, a.dtype) for a in arrays],
        in_specs=[pl.BlockSpec(memory_space=pltpu.VMEM)] * 3,
        out_specs=[pl.BlockSpec(memory_space=pltpu.HBM)] * 3,
        scratch_shapes=[pltpu.SemaphoreType.DMA((3,))],
        compiler_params=pltpu.CompilerParams(vmem_limit_bytes=48 * 1024 * 1024),
        name="copied",
    )(*arrays)


def where_am_i():
    tile = lax.axis_index("xy")
    return lax.axis_index("gz"), tile // 8, tile % 8


def per_device(
    left_vectors,
    sign_seeds,
    level_codes,
    level_table,
    disorder_sites,
    disorder_strength,
    hoppings,
    mass_raw,
):
    moments, prev, last = whole(
        where_am_i,
        True,
        sign_seeds,
        hoppings,
        mass_raw,
        level_codes.reshape(8, 128),
        level_table,
        disorder_sites.reshape(32, 128),
        disorder_strength.reshape(32, 128),
        left_vectors.reshape(3, 1024, 128),
    )
    moments, prev, last = copied(moments, prev, last)
    shape = left_vectors.shape[1:]
    return moments, prev.reshape(shape), last.reshape(shape)


def solution(mesh):
    in_specs = (
        P(None, None, None, "gz", "xy", None),
        P(),
        P("gz", "xy", None),
        P(),
        P(),
        P(),
        P(),
        P(),
    )
    out_specs = (P(), P(None, None, "gz", "xy", None), P(None, None, "gz", "xy", None))
    return jax.shard_map(
        per_device, mesh=mesh, in_specs=in_specs, out_specs=out_specs, check_vma=False
    )
```
